128 devices in a mesh: rows: 16 (over z, y), cols: 8 (over x, core).
Axes of the slice: x: 4, y: 4, z: 4, core: 2. Of those that a mesh axis runs over, the one named last changes fastest.
Arguments:
- atm_field: bfloat16 [1024, 2048, 320], P('rows', 'cols'), may hold values from -6 to 6
- remap_weights: bfloat16 [2048, 3, 4, 64], P(('rows', 'cols')), may hold values from -1.75 to 1.75
- pair_owner: int32 [8192, 1], P(('rows', 'cols')), may hold values from 0 to 15; in each aligned block of 64 rows (0 to 63, 64 to 127, ...) at most 8 rows name the same one
- pair_local: int32 [8192], P(('rows', 'cols')), may hold values from 0 to 15
- pair_weight: int32 [8192], P(('rows', 'cols')), may hold values from 0 to 15
Outputs:
- remapped: bfloat16 [2048, 256, 320], P(('rows', 'cols'))
The draws below stay inside these ranges and needn't reach their ends.
Inputs may be any that keep to these rules, and one draw needn't show every extreme that they name: `pair_owner`: of the 64 pairs of one device, at most 8 name the same owner row, and some device has exactly 8 naming one row.
All inputs are finite; a program needn't handle non-finite values.
Results may differ from the reference program's by a relative error of at most 0.011.
Values may be sent and summed in bfloat16 or wider, within the bound.
No kernel may reach another device: no remote copies, remote signals or barrier semaphores. Data moves between devices by JAX's collectives and lax.ppermute only.
A program may use at most 192 MiB of HBM per device.

```python
import math
import jax
import jax.numpy as jnp
import numpy as np
from jax import lax

CHAN = 320
SIDE = 32
BX = 2
BY = 8
WDEV = 16
QCELL = 64
OB_DEV = 16
PAIRS_DEV = 64
CAP = 8
AX = 1024
AY = 2048
OBLOCKS = 2048
PAIRS = 8192
WBLK = 2048
N_ROWS = 16
N_COLS = 8


def set_ends(result, own_key, least, largest):
    extent = result.shape
    place = [jax.random.randint(jax.random.fold_in(own_key, axis), (), 0, extent[axis]) for axis in range(len(extent))]
    result = result.at[tuple(place)].set(least)
    longest = extent.index(max(extent))
    place[longest] = (place[longest] + 1) % extent[longest]
    return result.at[tuple(place)].set(largest)


def steps_of(stream_key, dims, cuts, least, top_value):
    loudness = 1.0
    for axis_at, parts in cuts:
        heights = jax.random.uniform(jax.random.fold_in(jax.random.fold_in(stream_key, 6), axis_at), (parts,), jnp.float32, least / len(cuts), top_value / len(cuts))
        loudness = loudness * jnp.repeat(jnp.exp(heights), dims[axis_at] // parts).reshape((-1,) + (1,) * (len(dims) - 1 - axis_at))
    return loudness


def assign_block(own_key, own, number, rows, amount, top, most, lean):
    ranking = jax.random.permutation(own_key, amount)
    heavy_load, usual = portions_of(amount, rows * top, most, lean, True), portions_of(amount, rows * top, most, lean, False)
    places = jnp.arange(amount)

    def named(lengths, offset_by):
        used = int((lengths > 0).sum())
        fixed = max(1, used // 4)
        passed = fixed + (places - fixed + offset_by * (used - fixed)) % max(1, amount - fixed)
        return jnp.zeros((amount,), jnp.int32).at[ranking[jnp.where(places < fixed, places, passed)]].set(jnp.asarray(lengths, jnp.int32))

    lengths = jnp.where(number % 4 == 0, named(heavy_load, number // 4), named(usual, number - number // 4 - 1))
    mixed = jax.random.permutation(jax.random.fold_in(own, 3), amount)
    source_of, sink = mixed[0:amount // 2 * 2:2], mixed[1:amount // 2 * 2:2]
    margin = jnp.minimum(lengths[source_of] - 1, most - lengths[sink]) // 2
    margin = jnp.where((source_of == ranking[0]) | (sink == ranking[0]) | (lengths[sink] == 0), 0, jnp.maximum(margin, 0))
    passed = jax.random.randint(jax.random.fold_in(own, 4), (amount // 2,), 0, 1 << 20) % (margin + 1)
    lengths = lengths.at[source_of].add(-passed).at[sink].add(passed)
    members = jnp.searchsorted(jnp.cumsum(lengths), jnp.arange(rows * top), side="right").astype(jnp.int32)
    listing = members.reshape(top, rows).T
    listing = listing[jax.random.permutation(jax.random.fold_in(own, 1), rows)]
    offset_by = jax.random.randint(jax.random.fold_in(own, 2), (rows, 1), 0, top)
    return jnp.take_along_axis(listing, (jnp.arange(top)[None, :] + offset_by) % top, axis=1)


def portions_of(amount, total, most, skew, full):
    loads = [(1 << 20) // math.isqrt(grade ** skew) + 1 for grade in range(1, amount + 1)]
    largest = most if full else min(most, max(-(-total // amount), total * loads[0] // sum(loads)))
    least = 1 if total - largest >= amount - 1 else 0
    holding, spare = [largest] + [least] * (amount - 1), total - largest - least * (amount - 1)
    while spare > 0:
        movable = [i for i in range(1, amount) if holding[i] < largest] or [i for i in range(1, amount) if holding[i] < most]
        mass, budget = sum([loads[i] for i in movable]), spare
        for i in movable:
            extra = min(most - holding[i], max(1, budget * loads[i] // mass), spare)
            holding[i] = holding[i] + extra
            spare = spare - extra
    return np.array(holding)


def noise(key, shape, scale, most, cuts=(), held_as=jnp.bfloat16):
    entries = scale * jax.random.normal(key, shape, jnp.float32)
    if cuts:
        entries = entries * steps_of(key, shape, cuts, -0.22, 0.18)
    return jnp.clip(entries, -most, most).astype(held_as)


def setup_inputs(seed: int = 0) -> dict:
    key_list = jax.random.split(jax.random.key(seed), 6)
    atm_field = noise(key_list[0], (AX, AY, CHAN), 1.0, 6.0, ((0, 16), (1, 8)))
    remap_weights = noise(key_list[1], (WBLK, 3, 4, QCELL), 12 ** -0.5, 1.75, ((0, 128),))
    pair_owner_keys = jax.random.split(jax.random.fold_in(key_list[2], 1), PAIRS // PAIRS_DEV)
    pair_owner_turns = jax.random.permutation(jax.random.fold_in(key_list[2], 3), PAIRS // PAIRS_DEV)
    pair_owner = jax.vmap(lambda own, number: assign_block(jax.random.fold_in(key_list[2], 2), own, number, PAIRS_DEV, N_ROWS, 1, CAP, 2))(pair_owner_keys, pair_owner_turns).reshape((PAIRS, 1))
    pair_local = set_ends(jax.random.randint(key_list[3], (PAIRS,), 0, OB_DEV), jax.random.fold_in(key_list[3], 1), 0, OB_DEV - 1).astype(jnp.int32)
    pair_weight = set_ends(jax.random.randint(key_list[4], (PAIRS,), 0, WDEV), jax.random.fold_in(key_list[4], 1), 0, WDEV - 1).astype(jnp.int32)
    return {"atm_field": atm_field, "remap_weights": remap_weights, "pair_owner": pair_owner, "pair_local": pair_local, "pair_weight": pair_weight}


def bounded_take(field, begin, count, limit, axis):
    positions = begin + jnp.arange(count, dtype=jnp.int32)
    inside = ((positions >= 0) & (positions < limit)).astype(field.dtype)
    gathered = jnp.take(field, jnp.clip(positions, 0, limit - 1), axis=axis)
    if axis == 0:
        return gathered * inside[:, None, None]
    return gathered * inside[None, :, None]


def quarterize(field_cells, blocks_first, blocks_second):
    channels = field_cells.shape[-1]
    half = SIDE // 4
    gridded = field_cells.reshape(blocks_first, 2, half, 2, blocks_second, 2, half, 2, channels)
    ordered = gridded.transpose(0, 4, 1, 5, 3, 7, 2, 6, 8)
    return ordered.reshape(blocks_first * blocks_second, 4, 4, half * half, channels)


def reference(atm_field, remap_weights, pair_owner, pair_local, pair_weight):
    height = BX * SIDE
    breadth = BY * SIDE
    block_count = BX * BY
    pairs_here = 4 * block_count
    quarter = SIDE * SIDE // 16
    total_rows = atm_field.shape[0]
    total_cols = atm_field.shape[1]
    channels = atm_field.shape[2]
    owners_all = pair_owner[:, 0]

    def device_step(carry, device):
        row_index = device // N_COLS
        col_index = device % N_COLS
        band_rows = bounded_take(atm_field, row_index * height - 1, height + 2, total_rows, 0)
        slab_cells = bounded_take(band_rows, col_index * breadth - 1, breadth + 2, total_cols, 1)
        centre = slab_cells[1:-1, 1:-1]
        grad_first = ((slab_cells[2:, 1:-1].astype(jnp.float32) - slab_cells[:-2, 1:-1].astype(jnp.float32)) * 0.5).astype(jnp.bfloat16)
        grad_second = ((slab_cells[1:-1, 2:].astype(jnp.float32) - slab_cells[1:-1, :-2].astype(jnp.float32)) * 0.5).astype(jnp.bfloat16)
        stacked = jnp.stack([quarterize(centre, BX, BY), quarterize(grad_first, BX, BY), quarterize(grad_second, BX, BY)], axis=1).astype(jnp.float32)
        weights = lax.dynamic_slice_in_dim(remap_weights, device * WDEV, WDEV, 0)
        choose_idx = lax.dynamic_slice_in_dim(pair_weight, device * pairs_here, pairs_here, 0)
        chosen = jnp.take(weights, choose_idx, axis=0).astype(jnp.float32).reshape(block_count, 4, 3, 4, quarter)
        pieces = jnp.einsum('bumko,bmukoc->buoc', chosen, stacked, precision=lax.Precision.HIGHEST).astype(jnp.bfloat16)
        owners = lax.dynamic_slice_in_dim(owners_all, device * pairs_here, pairs_here, 0)
        local_ids = lax.dynamic_slice_in_dim(pair_local, device * pairs_here, pairs_here, 0)
        target = (owners * N_COLS + col_index) * OB_DEV + local_ids
        quarter_idx = jnp.arange(pairs_here, dtype=jnp.int32) % 4
        carry = carry.at[target, quarter_idx].add(pieces.reshape(pairs_here, quarter, channels).astype(jnp.float32))
        return carry, None

    initial = jnp.zeros((OBLOCKS, 4, quarter, channels), jnp.float32)
    totals, unused = lax.scan(device_step, initial, jnp.arange(N_ROWS * N_COLS, dtype=jnp.int32))
    return totals.reshape(OBLOCKS, 4 * quarter, channels).astype(jnp.bfloat16)
```

```python
import functools

import jax
import jax.numpy as jnp
from jax import lax
from jax.experimental import pallas as pl
from jax.experimental.pallas import tpu as pltpu
from jax.sharding import PartitionSpec as P

LANES = 128
QUARTER = 16
OCEAN = 64
LABEL_ROWS = 16
VMEM_LIMIT = 48 * 1024 * 1024
SMEM = pl.BlockSpec(memory_space=pltpu.SMEM)
VMEM = pl.BlockSpec(memory_space=pltpu.VMEM)
ANY = pl.BlockSpec(memory_space=pl.ANY)


def lanes_of(shape):
    return lax.broadcasted_iota(jnp.int32, shape, 1)


def params():
    return pltpu.CompilerParams(vmem_limit_bytes=VMEM_LIMIT)


def edge_kernel(x_ref, first_ref, last_ref, slab, sem):
    rows, chan, cols = x_ref.shape
    chunk = rows // sem.shape[0]

    def load(k):
        at = pl.ds(k * chunk, chunk)
        return pltpu.make_async_copy(x_ref.at[at], slab.at[at], sem.at[k])

    for k in range(sem.shape[0]):
        load(k).start()
    half = chan // 2
    first_ref[...] = jnp.zeros_like(first_ref)
    last_ref[...] = jnp.zeros_like(last_ref)
    lane = lanes_of((half, LANES))
    for k in range(sem.shape[0]):
        load(k).wait()
        for part in range(2):
            at = slice(part * half, (part + 1) * half)

            def row(n, held):
                first, last = held
                r = k * chunk + n
                head = slab[r, at, 0:LANES].astype(jnp.float32)[:, 0:1]
                tail = slab[r, at, cols - LANES : cols].astype(jnp.float32)[:, LANES - 1 : LANES]
                return (
                    jnp.where(lane == r + LANES // 2, head, first),
                    jnp.where(lane == r, tail, last),
                )

            held = (first_ref[at, :].astype(jnp.float32), last_ref[at, :].astype(jnp.float32))
            first, last = lax.fori_loop(0, chunk, row, held)
            first_ref[at, :] = first.astype(jnp.bfloat16)
            last_ref[at, :] = last.astype(jnp.bfloat16)


def edges_of(x):
    rows, chan, cols = x.shape
    edge = jax.ShapeDtypeStruct((chan, LANES), jnp.bfloat16)
    return pl.pallas_call(
        edge_kernel,
        out_shape=(edge, edge),
        in_specs=[ANY],
        out_specs=(VMEM, VMEM),
        scratch_shapes=[pltpu.VMEM(x.shape, jnp.bfloat16), pltpu.SemaphoreType.DMA((4,))],
        compiler_params=params(),
        cost_estimate=pl.CostEstimate(flops=1_000_000, bytes_accessed=x.size * 2, transcendentals=0),
        name="edges",
    )(x)


def halo_of(x):
    n_rows, n_cols = lax.axis_size("rows"), lax.axis_size("cols")
    up = [(i, i + 1) for i in range(n_rows - 1)]
    down = [(i + 1, i) for i in range(n_rows - 1)]
    right = [(i, i + 1) for i in range(n_cols - 1)]
    left = [(i + 1, i) for i in range(n_cols - 1)]
    top = lax.ppermute(x[-1], "rows", up)
    bottom = lax.ppermute(x[0], "rows", down)
    first, last = edges_of(x)
    west = lax.ppermute(last, "cols", right)
    east = lax.ppermute(first, "cols", left)
    return top, bottom, west, east


def expand(masks, rows):
    total = jnp.zeros(masks[0].shape, jnp.float32)
    for mask, row in zip(masks, rows):
        total = jnp.where(mask, row, total)
    return total.astype(jnp.bfloat16)


def split(value):
    high = value.astype(jnp.bfloat16).astype(jnp.float32)
    return high, value - high


def piece_kernel(
    capacity,
    owner_ref,
    local_ref,
    weight_ref,
    choice_ref,
    x_ref,
    top_ref,
    bottom_ref,
    west_ref,
    east_ref,
    out_ref,
    slab,
    matrix,
    held,
    stage,
    labels,
    at_ref,
    count_ref,
    in_sem,
    out_sem,
):
    rows, chan, cols = x_ref.shape
    bands, across = rows // QUARTER, cols // QUARTER
    pairs = bands * across
    peers = out_ref.shape[0]
    piece_rows = stage.shape[1]
    half = chan // 2

    def load(band):
        return pltpu.make_async_copy(
            x_ref.at[pl.ds(band * QUARTER, QUARTER)],
            slab.at[pl.ds(1 + band * QUARTER, QUARTER)],
            in_sem.at[band],
        )

    for band in range(bands):
        load(band).start()
    rims = [
        pltpu.make_async_copy(top_ref, slab.at[0], in_sem.at[bands]),
        pltpu.make_async_copy(bottom_ref, slab.at[rows + 1], in_sem.at[bands + 1]),
    ]
    for rim in rims:
        rim.start()

    for p in range(peers):
        count_ref[p] = 0

    def assign(q, table):
        owner = owner_ref[q]
        taken = count_ref[owner]
        at_ref[q] = taken * piece_rows
        count_ref[owner] = taken + 1
        here = (lax.broadcasted_iota(jnp.int32, table.shape, 0) == owner) & (
            lanes_of(table.shape) == taken
        )
        return jnp.where(here, local_ref[q] * 4 + q % 4, table)

    table = lax.fori_loop(0, pairs, assign, jnp.full((peers, LANES), -1, jnp.int32))
    table = table.astype(jnp.float32)
    for p in range(peers):
        labels[p] = jnp.broadcast_to(table[p : p + 1], (LABEL_ROWS, LANES)).astype(jnp.bfloat16)
    label_copy = pltpu.make_async_copy(
        labels, out_ref.at[:, pl.ds(capacity * piece_rows, LABEL_ROWS), :], in_sem.at[bands + 2]
    )
    label_copy.start()

    matrix[...] = jnp.zeros_like(matrix)
    sides = west_ref[...] + east_ref[...]
    for rim in rims:
        rim.wait()
    load(0).wait()

    @pl.loop(0, bands)
    def _(qr):
        @pl.when(qr + 1 < bands)
        def _():
            load(qr + 1).wait()

        shape = (LANES, LANES)
        wj, lane = lax.broadcasted_iota(jnp.int32, shape, 0), lanes_of(shape)
        pick = (wj // 8 == choice_ref[pl.ds(qr, 1), :]) & (wj % 8 == lane % 8)
        weights = jnp.dot(
            weight_ref[...],
            pick.astype(jnp.float32).astype(jnp.bfloat16),
            preferred_element_type=jnp.float32,
        )
        for i in range(8):
            w = weights[16 * i : 16 * (i + 1)]
            if i:
                w = pltpu.roll(w, 8 * i, 1)
            value = [w[k : k + 1] for k in range(4)]
            first = [0.5 * w[4 + k : 5 + k] for k in range(4)]
            second = [0.5 * w[8 + k : 9 + k] for k in range(4)]
            shape = (cols, LANES)
            column = (lanes_of(shape) - 8 * i) & (LANES - 1)
            offset = lax.broadcasted_iota(jnp.int32, shape, 0) - 2 * column
            masks = [offset == 0, offset == 1, offset == -1, offset == 2]
            m = matrix.at[i % 2]
            m[0:cols, 0:LANES] = expand(masks[:2], [-first[0], -first[1]])
            m[3 * cols : 4 * cols, 0:LANES] = expand(masks[:2], [first[2], first[3]])
            for s in range(2):
                inner = [-first[2], -first[3]] if s == 0 else [first[0], first[1]]
                near = split(value[2 * s] + inner[0] - second[2 * s + 1])
                far = split(value[2 * s + 1] + inner[1] + second[2 * s])
                at = slice((1 + s) * cols, (2 + s) * cols)
                m[at, 0:LANES] = expand(
                    masks, [near[0], far[0], -second[2 * s], second[2 * s + 1]]
                )
                m[at, LANES:] = expand(masks[:2], [near[1], far[1]])
            shape = (LANES, LANES)
            column = (lanes_of(shape) - 8 * i) & (LANES - 1)
            source = lax.broadcasted_iota(jnp.int32, shape, 0)
            base = 16 * qr + 2 * i
            rim_masks, rim_rows = [], []
            for s in range(2):
                rim_masks += [
                    (source == base + s) & (column == 0),
                    (source == base + s + LANES // 2) & (column == LANES - 1),
                ]
                rim_rows += [-second[2 * s], second[2 * s + 1]]
            m[4 * cols :, 0:LANES] = expand(rim_masks, rim_rows)
            cells = jnp.concatenate([slab[base + n] for n in range(4)] + [sides], axis=1)
            both = jnp.dot(cells, m[...], preferred_element_type=jnp.float32)
            held[i] = both[:, 0:LANES] + both[:, LANES:]

        shape = (half, LANES)
        group = lanes_of(shape) // 8
        for qc in range(8):
            turn = (group - qc) & 7
            lower, upper = held[0, 0:half], held[0, half:]
            for i in range(1, 8):
                lower = jnp.where(turn == i, held[i, 0:half], lower)
                upper = jnp.where(turn == i, held[i, half:], upper)
            early = ((group - qc) & 15) < 8
            both = (
                jnp.where(early, lower, pltpu.roll(upper, LANES // 2, 1)),
                jnp.where(early, pltpu.roll(lower, LANES // 2, 1), upper),
            )
            for n, piece in enumerate(both):
                column = qc + 8 * n
                q = ((qr // 2) * (across // 2) + column // 2) * 4 + (qr % 2) * 2 + column % 2
                if qc:
                    piece = pltpu.roll(piece, LANES - 8 * qc, 1)
                stage[q] = piece.astype(jnp.bfloat16)
                at = pl.multiple_of(at_ref[q], 16)
                pltpu.make_async_copy(
                    stage.at[q], out_ref.at[owner_ref[q], pl.ds(at, piece_rows)], out_sem
                ).start()

    label_copy.wait()
    for q in range(pairs):
        pltpu.make_async_copy(stage.at[q], out_ref.at[0, pl.ds(0, piece_rows)], out_sem).wait()


def make_pieces(x, halo, remap_weights, owners, locals_, choices, peers, capacity):
    rows, chan, cols = x.shape
    pairs = owners.shape[0]
    bands, across = rows // QUARTER, cols // QUARTER
    piece_rows = OCEAN * chan // LANES
    blocks = remap_weights.shape[0]
    weights = remap_weights.reshape(blocks, 12, 8, 8).transpose(2, 1, 0, 3)
    weights = jnp.pad(weights, ((0, 0), (0, 4), (0, 0), (0, 0))).reshape(LANES, blocks * 8)
    choice = choices.reshape(bands // 2, across // 2, 2, 2).transpose(0, 2, 1, 3)
    choice = jnp.repeat(choice.reshape(bands, across), 8, axis=1)
    return pl.pallas_call(
        functools.partial(piece_kernel, capacity),
        out_shape=jax.ShapeDtypeStruct(
            (peers, capacity * piece_rows + LABEL_ROWS, LANES), jnp.bfloat16
        ),
        in_specs=[SMEM, SMEM, VMEM, VMEM, ANY, ANY, ANY, VMEM, VMEM],
        out_specs=ANY,
        scratch_shapes=[
            pltpu.VMEM((rows + 2, chan, cols), jnp.bfloat16),
            pltpu.VMEM((2, 4 * cols + LANES, 2 * LANES), jnp.bfloat16),
            pltpu.VMEM((8, chan, LANES), jnp.float32),
            pltpu.VMEM((pairs, piece_rows, LANES), jnp.bfloat16),
            pltpu.VMEM((peers, LABEL_ROWS, LANES), jnp.bfloat16),
            pltpu.SMEM((pairs,), jnp.int32),
            pltpu.SMEM((peers,), jnp.int32),
            pltpu.SemaphoreType.DMA((bands + 3,)),
            pltpu.SemaphoreType.DMA,
        ],
        compiler_params=params(),
        cost_estimate=pl.CostEstimate(
            flops=4_000_000_000, bytes_accessed=16_000_000, transcendentals=0
        ),
        name="pieces",
    )(owners, locals_, weights, choice, x, *halo)


def sum_kernel(capacity, arrived_ref, out_ref, stage, label_vmem, label_smem, head, after, sem):
    blocks, chan, _ = out_ref.shape
    peers = arrived_ref.shape[0]
    half = chan // 2
    at = capacity * half
    found = arrived_ref[:, at : at + LABEL_ROWS, :].astype(jnp.float32)
    label_vmem[...] = jnp.max(found, axis=1).astype(jnp.int32)
    copy = pltpu.make_async_copy(label_vmem, label_smem, sem)
    copy.start()

    @pl.loop(0, 4 * blocks)
    def _(t):
        head[t] = -1

    copy.wait()

    @pl.loop(0, peers)
    def _(p):
        for k in range(capacity):
            target = label_smem[p, k]

            @pl.when(target >= 0)
            def _():
                slot = p * capacity + k
                after[slot] = head[target]
                head[target] = slot

    early = lanes_of((half, LANES)) < LANES // 2

    @pl.loop(0, blocks)
    def _(block):
        for pair in range(2):
            sums = []
            for n in range(2):

                def more(held):
                    return held[0] >= 0

                def add(held):
                    slot, total = held
                    start = pl.multiple_of((slot % capacity) * half, 16)
                    piece = arrived_ref[slot // capacity, pl.ds(start, half), :]
                    return after[slot], total + piece.astype(jnp.float32)

                start = head[block * 4 + pair * 2 + n]
                sums.append(
                    lax.while_loop(more, add, (start, jnp.zeros((half, LANES), jnp.float32)))[1]
                )
            turned = [pltpu.roll(total, LANES // 2, 1) for total in sums]
            at = slice(pair * LANES, (pair + 1) * LANES)
            stage[block, 0:half, at] = jnp.where(early, sums[0], turned[1]).astype(jnp.bfloat16)
            stage[block, half:, at] = jnp.where(early, turned[0], sums[1]).astype(jnp.bfloat16)
        pltpu.make_async_copy(stage.at[block], out_ref.at[block], sem).start()

    pltpu.make_async_copy(stage, out_ref, sem).wait()


def sum_arrived(arrived, blocks, chan, capacity):
    peers = arrived.shape[0]
    return pl.pallas_call(
        functools.partial(sum_kernel, capacity),
        out_shape=jax.ShapeDtypeStruct((blocks, chan, 4 * OCEAN), jnp.bfloat16),
        in_specs=[VMEM],
        out_specs=ANY,
        scratch_shapes=[
            pltpu.VMEM((blocks, chan, 4 * OCEAN), jnp.bfloat16),
            pltpu.VMEM((peers, LANES), jnp.int32),
            pltpu.SMEM((peers, LANES), jnp.int32),
            pltpu.SMEM((4 * blocks,), jnp.int32),
            pltpu.SMEM((peers * capacity,), jnp.int32),
            pltpu.SemaphoreType.DMA,
        ],
        compiler_params=params(),
        cost_estimate=pl.CostEstimate(flops=10_000_000, bytes_accessed=8_000_000, transcendentals=0),
        name="sum_arrived",
    )(arrived)


def per_device(atm_field, remap_weights, pair_owner, pair_local, pair_weight):
    rows, cols, chan = atm_field.shape
    pairs = pair_local.shape[0]
    peers = lax.axis_size("rows")
    capacity = 2 * pairs // peers
    x = atm_field.transpose(0, 2, 1)
    halo = halo_of(x)
    outgoing = make_pieces(
        x, halo, remap_weights, pair_owner[:, 0], pair_local, pair_weight, peers, capacity
    )
    arrived = lax.all_to_all(outgoing, "rows", split_axis=0, concat_axis=0, tiled=True)
    return sum_arrived(arrived, pairs // 4, chan, capacity).transpose(0, 2, 1)


def solution(mesh):
    placed = (
        P("rows", "cols", None),
        P(("rows", "cols"), None, None, None),
        P(("rows", "cols"), None),
        P(("rows", "cols")),
        P(("rows", "cols")),
    )
    return jax.shard_map(
        per_device,
        mesh=mesh,
        in_specs=placed,
        out_specs=P(("rows", "cols"), None, None),
        check_vma=False,
    )
```

```python
import functools

import jax
import jax.numpy as jnp
from jax import lax
from jax.experimental import pallas as pl
from jax.experimental.pallas import tpu as pltpu
from jax.sharding import PartitionSpec as P

LANES = 128
QUARTER = 16
OCEAN = 64
LABEL_ROWS = 16
MIB = 1024 * 1024
SMEM = pl.BlockSpec(memory_space=pltpu.SMEM)
VMEM = pl.BlockSpec(memory_space=pltpu.VMEM)
HBM = pl.BlockSpec(memory_space=pltpu.HBM)


def lanes_of(shape):
    return lax.broadcasted_iota(jnp.int32, shape, 1)


def params(mib):
    return pltpu.CompilerParams(vmem_limit_bytes=mib * MIB)


def edge_kernel(
    capacity,
    owner_ref,
    local_ref,
    x_ref,
    first_ref,
    last_ref,
    edge_ref,
    at_ref,
    label_ref,
    slab_ref,
    pick,
    count_ref,
    sem,
):
    rows, chan, cols = x_ref.shape
    parts = sem.shape[0]
    chunk = rows // parts

    def load(k):
        at = pl.ds(k * chunk, chunk)
        return pltpu.make_async_copy(x_ref.at[at], slab_ref.at[at], sem.at[k])

    for k in range(parts):
        load(k).start()
    shape = (cols, LANES)
    column, lane = lax.broadcasted_iota(jnp.int32, shape, 0), lanes_of(shape)
    for n in range(8):
        wanted = ((column == cols - 1) & (lane == n)) | ((column == 0) & (lane == LANES // 2 + n))
        pick[n * cols : (n + 1) * cols] = wanted.astype(jnp.float32).astype(jnp.bfloat16)

    peers = label_ref.shape[0]
    piece_rows = OCEAN * chan // LANES
    for p in range(peers):
        count_ref[p] = 0

    def assign(q, table):
        owner = owner_ref[q]
        taken = count_ref[owner]
        at_ref[q] = owner * (capacity * piece_rows + LABEL_ROWS) + taken * piece_rows
        count_ref[owner] = taken + 1
        here = (lax.broadcasted_iota(jnp.int32, table.shape, 0) == owner) & (
            lanes_of(table.shape) == taken
        )
        return jnp.where(here, local_ref[q] * 4 + q % 4, table)

    table = lax.fori_loop(
        0, owner_ref.shape[0], assign, jnp.full((peers, LANES), -1, jnp.int32)
    ).astype(jnp.float32)
    for p in range(peers):
        label_ref[p] = jnp.broadcast_to(table[p : p + 1], (LABEL_ROWS, LANES)).astype(jnp.bfloat16)

    total = jnp.zeros((chan, LANES), jnp.float32)
    for g in range(rows // 8):
        if 8 * g % chunk == 0:
            load(8 * g // chunk).wait()
        cells = jnp.concatenate([slab_ref[8 * g + n] for n in range(8)], axis=1)
        found = jnp.dot(cells, pick[...], preferred_element_type=jnp.float32)
        total = total + (pltpu.roll(found, 8 * g, 1) if g else found)
    edge_ref[...] = total.astype(jnp.bfloat16)
    first_ref[...] = slab_ref[0]
    last_ref[...] = slab_ref[rows - 1]


def find_edges(x, owners, locals_, peers, capacity):
    rows, chan, cols = x.shape
    row = jax.ShapeDtypeStruct((chan, cols), jnp.bfloat16)
    return pl.pallas_call(
        functools.partial(edge_kernel, capacity),
        out_shape=(
            row,
            row,
            jax.ShapeDtypeStruct((chan, LANES), jnp.bfloat16),
            jax.ShapeDtypeStruct(owners.shape, jnp.int32),
            jax.ShapeDtypeStruct((peers, LABEL_ROWS, LANES), jnp.bfloat16),
        ),
        in_specs=[SMEM, SMEM, HBM],
        out_specs=(VMEM, VMEM, VMEM, SMEM, VMEM),
        scratch_shapes=[
            pltpu.VMEM(x.shape, jnp.bfloat16),
            pltpu.VMEM((8 * cols, LANES), jnp.bfloat16),
            pltpu.SMEM((peers,), jnp.int32),
            pltpu.SemaphoreType.DMA((4,)),
        ],
        compiler_params=params(48),
        cost_estimate=pl.CostEstimate(flops=1_000_000, bytes_accessed=x.size * 2, transcendentals=0),
        name="find_edges",
    )(owners, locals_, x)


def halo_of(first, last, edge):
    n_rows, n_cols = lax.axis_size("rows"), lax.axis_size("cols")
    up = [(i, i + 1) for i in range(n_rows - 1)]
    down = [(i + 1, i) for i in range(n_rows - 1)]
    right = [(i, i + 1) for i in range(n_cols - 1)]
    left = [(i + 1, i) for i in range(n_cols - 1)]
    top = lax.ppermute(last, "rows", up)
    bottom = lax.ppermute(first, "rows", down)
    west = lax.ppermute(edge, "cols", right)
    east = lax.ppermute(edge, "cols", left)
    return top, bottom, west, east


def expand(masks, rows):
    total = jnp.zeros(masks[0].shape, jnp.float32)
    for mask, row in zip(masks, rows):
        total = jnp.where(mask, row, total)
    return total.astype(jnp.bfloat16)


def split(value):
    high = value.astype(jnp.bfloat16).astype(jnp.float32)
    return high, value - high


def fill_matrix(m, weights, i, base):
    cols = (m.shape[0] - LANES) // 4
    w = weights[16 * i : 16 * (i + 1)]
    if i:
        w = pltpu.roll(w, 8 * i, 1)
    value = [w[k : k + 1] for k in range(4)]
    first = [0.5 * w[4 + k : 5 + k] for k in range(4)]
    second = [0.5 * w[8 + k : 9 + k] for k in range(4)]
    shape = (cols, LANES)
    column = (lanes_of(shape) - 8 * i) & (LANES - 1)
    offset = lax.broadcasted_iota(jnp.int32, shape, 0) - 2 * column
    masks = [offset == 0, offset == 1, offset == -1, offset == 2]
    for s in range(2):
        inner = [-first[2], -first[3]] if s == 0 else [first[0], first[1]]
        near = split(value[2 * s] + inner[0] - second[2 * s + 1])
        far = split(value[2 * s + 1] + inner[1] + second[2 * s])
        at = slice(s * cols, (s + 1) * cols)
        m[at, 0:LANES] = expand(masks, [near[0], far[0], -second[2 * s], second[2 * s + 1]])
        m[at, LANES:] = expand(masks[:2], [near[1], far[1]])
    m[2 * cols : 3 * cols, 0:LANES] = expand(masks[:2], [-first[0], -first[1]])
    m[3 * cols : 4 * cols, 0:LANES] = expand(masks[:2], [first[2], first[3]])
    shape = (LANES, LANES)
    column = (lanes_of(shape) - 8 * i) & (LANES - 1)
    source = lax.broadcasted_iota(jnp.int32, shape, 0)
    rim_masks, rim_rows = [], []
    for s in range(2):
        rim_masks += [
            (source == base + s) & (column == 0),
            (source == base + s + LANES // 2) & (column == LANES - 1),
        ]
        rim_rows += [-second[2 * s], second[2 * s + 1]]
    m[4 * cols :, 0:LANES] = expand(rim_masks, rim_rows)


def gather_quarters(held, chunk, places, out_ref):
    half = held.shape[1] // 2
    group = lanes_of((QUARTER, LANES)) // 8
    mixed = []
    for part in range(2):
        start = part * half + chunk * QUARTER
        lines = [held[i, start : start + QUARTER] for i in range(8)]
        for bit in (1, 2, 4):
            on = (group & bit) != 0
            lines = [jnp.where(on, lines[(n + bit) % 8], lines[n]) for n in range(8)]
        mixed.append(lines)
    for qc in range(8):
        lower, upper = mixed[0][-qc % 8], mixed[1][-qc % 8]
        early = ((group - qc) & 15) < 8
        both = (jnp.where(early, lower, upper), jnp.where(early, upper, lower))
        for n, piece in enumerate(both):
            turn = (LANES - 8 * qc + n * LANES // 2) % LANES
            if turn:
                piece = pltpu.roll(piece, turn, 1)
            at = pl.multiple_of(places[qc + 8 * n] + chunk * QUARTER, QUARTER)
            out_ref[pl.ds(at, QUARTER), :] = piece.astype(jnp.bfloat16)


def piece_kernel(
    at_ref,
    label_ref,
    weight_ref,
    choice_ref,
    x_ref,
    top_ref,
    bottom_ref,
    west_ref,
    east_ref,
    out_ref,
    slab,
    above,
    below,
    matrix,
    held,
    sem,
):
    rows, chan, cols = x_ref.shape
    bands, across = rows // QUARTER, cols // QUARTER
    peers = label_ref.shape[0]
    peer_rows = out_ref.shape[0] // peers
    half = chan // 2
    chunks = half // QUARTER

    def load(band):
        start, stop = band * QUARTER + min(band, 1), min((band + 1) * QUARTER + 1, rows)
        cuts = [start + (stop - start) * n // 4 for n in range(5)]
        spans = [pl.ds(low, high - low) for low, high in zip(cuts[:-1], cuts[1:])]
        return [
            pltpu.make_async_copy(x_ref.at[at], slab.at[at], sem.at[band, n])
            for n, at in enumerate(spans)
        ]

    def begin(band):
        for copy in load(band):
            copy.start()

    def finish(band):
        for copy in load(band):
            copy.wait()

    begin(0)
    for p in range(peers):
        out_ref[(p + 1) * peer_rows - LABEL_ROWS : (p + 1) * peer_rows, :] = label_ref[p]
    matrix[...] = jnp.zeros_like(matrix)
    west = lanes_of(west_ref.shape) < LANES // 2
    sides = jnp.where(west, west_ref[...].astype(jnp.float32), east_ref[...].astype(jnp.float32))
    sides = sides.astype(jnp.bfloat16)
    finish(0)
    begin(1)

    @pl.loop(0, bands)
    def _(band):
        for b in range(1, bands):

            @pl.when(band == b)
            def _():
                finish(b)
                if b + 1 < bands:
                    begin(b + 1)

        above[...] = jnp.where(band == 0, top_ref[...], slab[jnp.maximum(band * QUARTER - 1, 0)])
        following = jnp.minimum((band + 1) * QUARTER, rows - 1)
        below[...] = jnp.where(band == bands - 1, bottom_ref[...], slab[following])

        shape = (LANES, LANES)
        wj, lane = lax.broadcasted_iota(jnp.int32, shape, 0), lanes_of(shape)
        pick = (wj // 8 == choice_ref[pl.ds(band, 1), :]) & (wj % 8 == lane % 8)
        weights = jnp.dot(
            weight_ref[...],
            pick.astype(jnp.float32).astype(jnp.bfloat16),
            preferred_element_type=jnp.float32,
        )
        for i in range(8):
            base = QUARTER * band + 2 * i
            fill_matrix(matrix.at[i % 2], weights, i, base)
            cells = [
                slab[base],
                slab[base + 1],
                slab[base - 1] if i else above[...],
                slab[base + 2] if i < 7 else below[...],
                sides,
            ]
            both = jnp.dot(
                jnp.concatenate(cells, axis=1),
                matrix[i % 2],
                preferred_element_type=jnp.float32,
            )
            both = both[:, 0:LANES] + both[:, LANES:]
            held[i, 0:half] = both[0:half]
            held[i, half:] = pltpu.roll(both[half:], LANES // 2, 1)

        start = (band // 2) * (across // 2) * 4 + (band % 2) * 2
        places = [at_ref[start + (column // 2) * 4 + column % 2] for column in range(across)]
        for chunk in range(chunks):
            gather_quarters(held, chunk, places, out_ref)


def make_pieces(x, halo, remap_weights, slots, labels, choices, capacity):
    rows, chan, cols = x.shape
    peers = labels.shape[0]
    bands, across = rows // QUARTER, cols // QUARTER
    piece_rows = OCEAN * chan // LANES
    blocks = remap_weights.shape[0]
    weights = remap_weights.reshape(blocks, 12, 8, 8).transpose(2, 1, 0, 3)
    weights = jnp.pad(weights, ((0, 0), (0, 4), (0, 0), (0, 0))).reshape(LANES, blocks * 8)
    choice = choices.reshape(bands // 2, across // 2, 2, 2).transpose(0, 2, 1, 3)
    choice = jnp.repeat(choice.reshape(bands, across), 8, axis=1)
    return pl.pallas_call(
        piece_kernel,
        out_shape=jax.ShapeDtypeStruct(
            (peers * (capacity * piece_rows + LABEL_ROWS), LANES), jnp.bfloat16
        ),
        in_specs=[SMEM, VMEM, VMEM, VMEM, HBM, VMEM, VMEM, VMEM, VMEM],
        out_specs=VMEM,
        scratch_shapes=[
            pltpu.VMEM(x.shape, jnp.bfloat16),
            pltpu.VMEM((chan, cols), jnp.bfloat16),
            pltpu.VMEM((chan, cols), jnp.bfloat16),
            pltpu.VMEM((2, 4 * cols + LANES, 2 * LANES), jnp.bfloat16),
            pltpu.VMEM((8, chan, LANES), jnp.float32),
            pltpu.SemaphoreType.DMA((bands, 4)),
        ],
        compiler_params=params(48),
        cost_estimate=pl.CostEstimate(
            flops=4_000_000_000, bytes_accessed=16_000_000, transcendentals=0
        ),
        name="pieces",
    )(slots, labels, weights, choice, x, *halo)


def sum_kernel(capacity, arrived_ref, out_ref, stage, label_vmem, label_smem, head, after, sem):
    blocks, chan, _ = out_ref.shape
    peers = arrived_ref.shape[0]
    half = chan // 2
    at = capacity * half
    found = arrived_ref[:, at : at + LABEL_ROWS, :].astype(jnp.float32)
    label_vmem[...] = jnp.max(found, axis=1).astype(jnp.int32)
    copy = pltpu.make_async_copy(label_vmem, label_smem, sem)
    copy.start()

    @pl.loop(0, 4 * blocks)
    def _(t):
        head[t] = -1

    copy.wait()

    @pl.loop(0, peers)
    def _(p):
        for k in range(capacity):
            target = label_smem[p, k]

            @pl.when(target >= 0)
            def _():
                slot = p * capacity + k
                after[slot] = head[target]
                head[target] = slot

    early = lanes_of((half, LANES)) < LANES // 2

    @pl.loop(0, blocks)
    def _(block):
        for pair in range(2):
            sums = []
            for n in range(2):

                def more(held):
                    return held[0] >= 0

                def add(held):
                    slot, total = held
                    start = pl.multiple_of((slot % capacity) * half, 16)
                    piece = arrived_ref[slot // capacity, pl.ds(start, half), :]
                    return after[slot], total + piece.astype(jnp.float32)

                start = head[block * 4 + pair * 2 + n]
                sums.append(
                    lax.while_loop(more, add, (start, jnp.zeros((half, LANES), jnp.float32)))[1]
                )
            turned = [pltpu.roll(total, LANES // 2, 1) for total in sums]
            at = slice(pair * LANES, (pair + 1) * LANES)
            stage[block, 0:half, at] = jnp.where(early, sums[0], turned[1]).astype(jnp.bfloat16)
            stage[block, half:, at] = jnp.where(early, turned[0], sums[1]).astype(jnp.bfloat16)
        pltpu.make_async_copy(stage.at[block], out_ref.at[block], sem).start()

    pltpu.make_async_copy(stage, out_ref, sem).wait()


def sum_arrived(arrived, blocks, chan, capacity):
    peers = arrived.shape[0]
    return pl.pallas_call(
        functools.partial(sum_kernel, capacity),
        out_shape=jax.ShapeDtypeStruct((blocks, chan, 4 * OCEAN), jnp.bfloat16),
        in_specs=[VMEM],
        out_specs=HBM,
        scratch_shapes=[
            pltpu.VMEM((blocks, chan, 4 * OCEAN), jnp.bfloat16),
            pltpu.VMEM((peers, LANES), jnp.int32),
            pltpu.SMEM((peers, LANES), jnp.int32),
            pltpu.SMEM((4 * blocks,), jnp.int32),
            pltpu.SMEM((peers * capacity,), jnp.int32),
            pltpu.SemaphoreType.DMA,
        ],
        compiler_params=params(8),
        cost_estimate=pl.CostEstimate(flops=10_000_000, bytes_accessed=8_000_000, transcendentals=0),
        name="sum_arrived",
    )(arrived)


def per_device(atm_field, remap_weights, pair_owner, pair_local, pair_weight):
    rows, cols, chan = atm_field.shape
    pairs = pair_local.shape[0]
    peers = lax.axis_size("rows")
    capacity = 2 * pairs // peers
    x = atm_field.transpose(0, 2, 1)
    owners = pair_owner[:, 0]
    first, last, edge, slots, labels = find_edges(x, owners, pair_local, peers, capacity)
    outgoing = make_pieces(
        x,
        halo_of(first, last, edge),
        remap_weights,
        slots,
        labels,
        pair_weight,
        capacity,
    )
    outgoing = outgoing.reshape(peers, -1, LANES)
    arrived = lax.all_to_all(outgoing, "rows", split_axis=0, concat_axis=0, tiled=True)
    return sum_arrived(arrived, pairs // 4, chan, capacity).transpose(0, 2, 1)


def solution(mesh):
    placed = (
        P("rows", "cols", None),
        P(("rows", "cols"), None, None, None),
        P(("rows", "cols"), None),
        P(("rows", "cols")),
        P(("rows", "cols")),
    )
    return jax.shard_map(
        per_device,
        mesh=mesh,
        in_specs=placed,
        out_specs=P(("rows", "cols"), None, None),
        check_vma=False,
    )
```

```python
import functools

import jax
import jax.numpy as jnp
from jax import lax
from jax.experimental import pallas as pl
from jax.experimental.pallas import tpu as pltpu
from jax.sharding import PartitionSpec as P

LANES = 128
QUARTER = 16
OCEAN = 64
LABEL_ROWS = 16
MIB = 1024 * 1024
SMEM = pl.BlockSpec(memory_space=pltpu.SMEM)
VMEM = pl.BlockSpec(memory_space=pltpu.VMEM)
HBM = pl.BlockSpec(memory_space=pltpu.HBM)


def lanes_of(shape):
    return lax.broadcasted_iota(jnp.int32, shape, 1)


def params(mib):
    return pltpu.CompilerParams(vmem_limit_bytes=mib * MIB)


def edge_kernel(
    capacity,
    owner_ref,
    local_ref,
    x_ref,
    early_ref,
    late_ref,
    edge_ref,
    at_ref,
    label_ref,
    slab_ref,
    pick,
    count_ref,
    sem,
):
    rows, chan, cols = x_ref.shape
    parts = sem.shape[0]
    chunk = rows // parts

    def load(k):
        at = pl.ds(k * chunk, chunk)
        return pltpu.make_async_copy(x_ref.at[at], slab_ref.at[at], sem.at[k])

    for k in range(parts):
        load(k).start()
    shape = (cols, LANES)
    column, lane = lax.broadcasted_iota(jnp.int32, shape, 0), lanes_of(shape)
    for n in range(8):
        wanted = ((column == cols - 1) & (lane == n)) | ((column == 0) & (lane == LANES // 2 + n))
        pick[n * cols : (n + 1) * cols] = wanted.astype(jnp.float32).astype(jnp.bfloat16)

    peers = label_ref.shape[0]
    piece_rows = OCEAN * chan // LANES
    for p in range(peers):
        count_ref[p] = 0

    def assign(q, table):
        owner = owner_ref[q]
        taken = count_ref[owner]
        at_ref[q] = owner * (capacity * piece_rows + LABEL_ROWS) + taken * piece_rows
        count_ref[owner] = taken + 1
        here = (lax.broadcasted_iota(jnp.int32, table.shape, 0) == owner) & (
            lanes_of(table.shape) == taken
        )
        return jnp.where(here, local_ref[q] * 4 + q % 4, table)

    table = lax.fori_loop(
        0, owner_ref.shape[0], assign, jnp.full((peers, LANES), owner_ref.shape[0], jnp.int32)
    ).astype(jnp.float32)
    for p in range(peers):
        label_ref[p] = jnp.broadcast_to(table[p : p + 1], (LABEL_ROWS, LANES)).astype(jnp.bfloat16)

    total = jnp.zeros((chan, LANES), jnp.float32)
    for g in range(rows // 8):
        if 8 * g % chunk == 0:
            load(8 * g // chunk).wait()
        cells = jnp.concatenate([slab_ref[8 * g + n] for n in range(8)], axis=1)
        found = jnp.dot(cells, pick[...], preferred_element_type=jnp.float32)
        total = total + (pltpu.roll(found, 8 * g, 1) if g else found)
    edge_ref[...] = total.astype(jnp.bfloat16)
    last = jnp.where(is_even("rows"), rows - 1, 0)
    early_ref[...] = slab_ref[last]
    late_ref[...] = slab_ref[rows - 1 - last]


def find_edges(x, owners, locals_, peers, capacity):
    rows, chan, cols = x.shape
    row = jax.ShapeDtypeStruct((chan, cols), jnp.bfloat16)
    return pl.pallas_call(
        functools.partial(edge_kernel, capacity),
        out_shape=(
            row,
            row,
            jax.ShapeDtypeStruct((chan, LANES), jnp.bfloat16),
            jax.ShapeDtypeStruct(owners.shape, jnp.int32),
            jax.ShapeDtypeStruct((peers, LABEL_ROWS, LANES), jnp.bfloat16),
        ),
        in_specs=[SMEM, SMEM, HBM],
        out_specs=(VMEM, VMEM, VMEM, SMEM, VMEM),
        scratch_shapes=[
            pltpu.VMEM(x.shape, jnp.bfloat16),
            pltpu.VMEM((8 * cols, LANES), jnp.bfloat16),
            pltpu.SMEM((peers,), jnp.int32),
            pltpu.SemaphoreType.DMA((4,)),
        ],
        compiler_params=params(48),
        cost_estimate=pl.CostEstimate(flops=1_000_000, bytes_accessed=x.size * 2, transcendentals=0),
        name="find_edges",
    )(owners, locals_, x)


def swaps(axis):
    count = lax.axis_size(axis)
    pairs = [[(i, i + 1) for i in range(start, count - 1, 2)] for start in range(2)]
    return [some + [(b, a) for a, b in some] for some in pairs]


def is_even(axis):
    return lax.axis_index(axis) % 2 == 0


def expand(masks, rows):
    total = jnp.zeros(masks[0].shape, jnp.float32)
    for mask, row in zip(masks, rows):
        total = jnp.where(mask, row, total)
    return total.astype(jnp.bfloat16)


def split(value):
    high = value.astype(jnp.bfloat16).astype(jnp.float32)
    return high, value - high


def parts_of(w):
    value = [w[k : k + 1] for k in range(4)]
    first = [0.5 * w[4 + k : 5 + k] for k in range(4)]
    second = [0.5 * w[8 + k : 9 + k] for k in range(4)]
    return value, first, second


def fill_matrices(inner, outer, w, i):
    cols = outer.shape[0] // 2
    value, first, second = parts_of(w)
    shape = (cols, LANES)
    column = (lanes_of(shape) - 8 * i) & (LANES - 1)
    offset = lax.broadcasted_iota(jnp.int32, shape, 0) - 2 * column
    masks = [offset == 0, offset == 1, offset == -1, offset == 2]
    for s in range(2):
        across = [-first[2], -first[3]] if s == 0 else [first[0], first[1]]
        near = split(value[2 * s] + across[0] - second[2 * s + 1])
        far = split(value[2 * s + 1] + across[1] + second[2 * s])
        at = slice(s * cols, (s + 1) * cols)
        inner[at, 0:LANES] = expand(masks, [near[0], far[0], -second[2 * s], second[2 * s + 1]])
        inner[at, LANES:] = expand(masks[:2], [near[1], far[1]])
    outer[0:cols] = expand(masks[:2], [-first[0], -first[1]])
    outer[cols:] = expand(masks[:2], [first[2], first[3]])


def side_matrix(rows_of, band):
    shape = (LANES, LANES)
    source, lane = lax.broadcasted_iota(jnp.int32, shape, 0), lanes_of(shape)
    first = QUARTER * band + 2 * (lane // 8)
    last = LANES // 2 + QUARTER * band + 2 * (((lane + 1) & (LANES - 1)) // 8)
    total = jnp.zeros(shape, jnp.float32)
    for s in range(2):
        row = jnp.zeros((1, LANES), jnp.float32)
        at = lanes_of(row.shape)
        for i in range(8):
            _, _, second = parts_of(rows_of[i])
            row = jnp.where(at == 8 * i, -second[2 * s], row)
            row = jnp.where(at == (8 * i - 1) % LANES, second[2 * s + 1], row)
        here = ((lane % 8 == 0) & (source == first + s)) | ((lane % 8 == 7) & (source == last + s))
        total = jnp.where(here, row, total)
    return total.astype(jnp.bfloat16)


def gather_quarters(held, chunk, places, out_ref):
    half = held.shape[1] // 2
    group = lanes_of((QUARTER, LANES)) // 8
    mixed = []
    for part in range(2):
        start = part * half + chunk * QUARTER
        lines = [held[i, start : start + QUARTER] for i in range(8)]
        for bit in (1, 2, 4):
            on = (group & bit) != 0
            lines = [jnp.where(on, lines[(n + bit) % 8], lines[n]) for n in range(8)]
        mixed.append(lines)
    for qc in range(8):
        lower, upper = mixed[0][-qc % 8], mixed[1][-qc % 8]
        early = ((group - qc) & 15) < 8
        both = (jnp.where(early, lower, upper), jnp.where(early, upper, lower))
        for n, piece in enumerate(both):
            turn = (LANES - 8 * qc + n * LANES // 2) % LANES
            if turn:
                piece = pltpu.roll(piece, turn, 1)
            at = pl.multiple_of(places[qc + 8 * n] + chunk * QUARTER, QUARTER)
            out_ref[pl.ds(at, QUARTER), :] = piece.astype(jnp.bfloat16)


def piece_kernel(
    at_ref,
    choice_ref,
    label_ref,
    weight_ref,
    x_ref,
    early_ref,
    late_ref,
    early_side_ref,
    late_side_ref,
    out_ref,
    slab,
    above,
    below,
    inner,
    outer,
    weights_ref,
    held,
    sem,
):
    rows, chan, cols = x_ref.shape
    bands, across = rows // QUARTER, cols // QUARTER
    peers = label_ref.shape[0]
    peer_rows = out_ref.shape[0] // peers
    half = chan // 2
    chunks = half // QUARTER

    def load(band):
        start, stop = band * QUARTER + min(band, 1), min((band + 1) * QUARTER + 1, rows)
        cuts = [start + (stop - start) * n // 4 for n in range(5)]
        spans = [pl.ds(low, high - low) for low, high in zip(cuts[:-1], cuts[1:])]
        return [
            pltpu.make_async_copy(x_ref.at[at], slab.at[at], sem.at[band, n])
            for n, at in enumerate(spans)
        ]

    def begin(band):
        for copy in load(band):
            copy.start()

    def finish(band):
        for copy in load(band):
            copy.wait()

    begin(0)
    for p in range(peers):
        out_ref[(p + 1) * peer_rows - LABEL_ROWS : (p + 1) * peer_rows, :] = label_ref[p]

    shape = (QUARTER, LANES)
    block = lanes_of(shape) // 8
    gathered = [jnp.zeros(shape, jnp.float32) for _ in range(8)]
    empty = jnp.zeros((4, OCEAN), jnp.float32)
    for n in range(weight_ref.shape[0]):
        terms = [weight_ref[n, m].astype(jnp.float32) for m in range(3)] + [empty]
        terms = jnp.concatenate(terms, axis=0)
        terms = jnp.concatenate([terms, jnp.zeros_like(terms)], axis=1)
        for i in range(8):
            turn = (8 * n - 8 * i) % LANES
            turned = pltpu.roll(terms, turn, 1) if turn else terms
            gathered[i] = jnp.where(block == n, turned, gathered[i])
    for i in range(8):
        weights_ref[QUARTER * i : QUARTER * (i + 1), :] = gathered[i].astype(jnp.bfloat16)

    even_row = is_even("rows")
    lane = lanes_of(early_side_ref.shape)
    take_early = (lane >= LANES // 2) == is_even("cols")
    sides = jnp.where(
        take_early, early_side_ref[...].astype(jnp.float32), late_side_ref[...].astype(jnp.float32)
    ).astype(jnp.bfloat16)
    finish(0)
    begin(1)

    @pl.loop(0, bands)
    def _(band):
        for b in range(1, bands):

            @pl.when(band == b)
            def _():
                finish(b)
                if b + 1 < bands:
                    begin(b + 1)

        above[...] = slab[jnp.maximum(band * QUARTER - 1, 0)]
        below[...] = slab[jnp.minimum((band + 1) * QUARTER, rows - 1)]

        @pl.when(band == 0)
        def _():
            above[...] = jnp.where(even_row, late_ref[...], early_ref[...])

        @pl.when(band == bands - 1)
        def _():
            below[...] = jnp.where(even_row, early_ref[...], late_ref[...])

        start = (band // 2) * (across // 2) * 4 + (band % 2) * 2
        pairs = [start + (column // 2) * 4 + column % 2 for column in range(across)]

        shape = (LANES, LANES)
        wj, lane = lax.broadcasted_iota(jnp.int32, shape, 0), lanes_of(shape)
        row = (1, LANES)
        choice = jnp.zeros(row, jnp.int32)
        for column, q in enumerate(pairs):
            choice = jnp.where(lanes_of(row) // 8 == column, choice_ref[q], choice)
        pick = (wj // 8 == choice) & (wj % 8 == lane % 8)
        weights = jnp.dot(
            weights_ref[...],
            pick.astype(jnp.float32).astype(jnp.bfloat16),
            preferred_element_type=jnp.float32,
        )
        rows_of = [weights[QUARTER * i : QUARTER * (i + 1)] for i in range(8)]
        rows_of = [pltpu.roll(w, 8 * i, 1) if i else w for i, w in enumerate(rows_of)]
        beside = jnp.dot(sides, side_matrix(rows_of, band), preferred_element_type=jnp.float32)
        for i in range(8):
            base = QUARTER * band + 2 * i
            fill_matrices(inner.at[i % 2], outer.at[i % 2], rows_of[i], i)
            own = jnp.dot(
                jnp.concatenate([slab[base], slab[base + 1]], axis=1),
                inner[i % 2],
                preferred_element_type=jnp.float32,
            )
            next_to = [slab[base - 1] if i else above[...], slab[base + 2] if i < 7 else below[...]]
            near = jnp.dot(
                jnp.concatenate(next_to, axis=1),
                outer[i % 2],
                preferred_element_type=jnp.float32,
            )
            lane = lanes_of(near.shape)
            rim = (lane == 8 * i) | (lane == (8 * i - 1) % LANES)
            total = (own[:, 0:LANES] + own[:, LANES:]) + (near + jnp.where(rim, beside, 0.0))
            held[i, 0:half] = total[0:half]
            held[i, half:] = pltpu.roll(total[half:], LANES // 2, 1)

        places = [at_ref[q] for q in pairs]
        for chunk in range(chunks):
            gather_quarters(held, chunk, places, out_ref)


def make_pieces(x, halo, remap_weights, slots, labels, choices, capacity):
    rows, chan, cols = x.shape
    peers = labels.shape[0]
    bands, across = rows // QUARTER, cols // QUARTER
    piece_rows = OCEAN * chan // LANES
    return pl.pallas_call(
        piece_kernel,
        out_shape=jax.ShapeDtypeStruct(
            (peers * (capacity * piece_rows + LABEL_ROWS), LANES), jnp.bfloat16
        ),
        in_specs=[SMEM, SMEM, VMEM, VMEM, HBM, VMEM, VMEM, VMEM, VMEM],
        out_specs=VMEM,
        scratch_shapes=[
            pltpu.VMEM(x.shape, jnp.bfloat16),
            pltpu.VMEM((chan, cols), jnp.bfloat16),
            pltpu.VMEM((chan, cols), jnp.bfloat16),
            pltpu.VMEM((2, 2 * cols, 2 * LANES), jnp.bfloat16),
            pltpu.VMEM((2, 2 * cols, LANES), jnp.bfloat16),
            pltpu.VMEM((LANES, LANES), jnp.bfloat16),
            pltpu.VMEM((8, chan, LANES), jnp.float32),
            pltpu.SemaphoreType.DMA((bands, 4)),
        ],
        compiler_params=params(48),
        cost_estimate=pl.CostEstimate(
            flops=4_000_000_000, bytes_accessed=16_000_000, transcendentals=0
        ),
        name="pieces",
    )(slots, choices, labels, remap_weights, x, *halo)


def sum_kernel(capacity, arrived_ref, out_ref, stage, label_vmem, label_smem, head, after, sem):
    blocks, chan, _ = out_ref.shape
    peers = label_vmem.shape[0]
    half = chan // 2
    peer_rows = arrived_ref.shape[0] // peers
    for p in range(peers):
        found = arrived_ref[(p + 1) * peer_rows - LABEL_ROWS : (p + 1) * peer_rows, :]
        label_vmem[p : p + 1] = found.astype(jnp.float32)[0:1].astype(jnp.int32)
    copy = pltpu.make_async_copy(label_vmem, label_smem, sem)
    copy.start()
    head[4 * blocks] = -1

    @pl.loop(0, 4 * blocks, unroll=8)
    def _(t):
        head[t] = -1

    copy.wait()

    @pl.loop(0, peers, unroll=4)
    def _(p):
        for k in range(capacity):
            target = label_smem[p, k]
            slot = p * (peer_rows // 16) + k * (half // 16)
            after[slot] = head[target]
            head[target] = slot

    early = lanes_of((half, LANES)) < LANES // 2

    @pl.loop(0, blocks)
    def _(block):
        for pair in range(2):
            sums = []
            for n in range(2):

                def more(held):
                    return held[0] >= 0

                def add(held):
                    slot, total = held
                    piece = arrived_ref[pl.ds(pl.multiple_of(slot * 16, 16), half), :]
                    return after[slot], total + piece.astype(jnp.float32)

                start = head[block * 4 + pair * 2 + n]
                sums.append(
                    lax.while_loop(more, add, (start, jnp.zeros((half, LANES), jnp.float32)))[1]
                )
            turned = [pltpu.roll(total, LANES // 2, 1) for total in sums]
            at = slice(pair * LANES, (pair + 1) * LANES)
            stage[block, 0:half, at] = jnp.where(early, sums[0], turned[1]).astype(jnp.bfloat16)
            stage[block, half:, at] = jnp.where(early, turned[0], sums[1]).astype(jnp.bfloat16)
        pltpu.make_async_copy(stage.at[block], out_ref.at[block], sem).start()

    pltpu.make_async_copy(stage, out_ref, sem).wait()


def sum_arrived(arrived, blocks, chan, peers, capacity):
    return pl.pallas_call(
        functools.partial(sum_kernel, capacity),
        out_shape=jax.ShapeDtypeStruct((blocks, chan, 4 * OCEAN), jnp.bfloat16),
        in_specs=[VMEM],
        out_specs=HBM,
        scratch_shapes=[
            pltpu.VMEM((blocks, chan, 4 * OCEAN), jnp.bfloat16),
            pltpu.VMEM((peers, LANES), jnp.int32),
            pltpu.SMEM((peers, LANES), jnp.int32),
            pltpu.SMEM((4 * blocks + 1,), jnp.int32),
            pltpu.SMEM((arrived.shape[0] // 16,), jnp.int32),
            pltpu.SemaphoreType.DMA,
        ],
        compiler_params=params(8),
        cost_estimate=pl.CostEstimate(flops=10_000_000, bytes_accessed=8_000_000, transcendentals=0),
        name="sum_arrived",
    )(arrived)


def per_device(atm_field, remap_weights, pair_owner, pair_local, pair_weight):
    rows, cols, chan = atm_field.shape
    pairs = pair_local.shape[0]
    peers = lax.axis_size("rows")
    capacity = 2 * pairs // peers
    x = atm_field.transpose(0, 2, 1)
    owners = pair_owner[:, 0]
    early, late, edge, slots, labels = find_edges(x, owners, pair_local, peers, capacity)
    halo = [lax.ppermute(row, "rows", swap) for row, swap in zip((early, late), swaps("rows"))]
    halo += [lax.ppermute(edge, "cols", swap) for swap in swaps("cols")]
    outgoing = make_pieces(
        x,
        halo,
        remap_weights,
        slots,
        labels,
        pair_weight,
        capacity,
    )
    outgoing = outgoing.reshape(peers, -1, LANES)
    arrived = lax.all_to_all(outgoing, "rows", split_axis=0, concat_axis=0, tiled=True)
    arrived = arrived.reshape(-1, LANES)
    return sum_arrived(arrived, pairs // 4, chan, peers, capacity).transpose(0, 2, 1)


def solution(mesh):
    placed = (
        P("rows", "cols", None),
        P(("rows", "cols"), None, None, None),
        P(("rows", "cols"), None),
        P(("rows", "cols")),
        P(("rows", "cols")),
    )
    return jax.shard_map(
        per_device,
        mesh=mesh,
        in_specs=placed,
        out_specs=P(("rows", "cols"), None, None),
        check_vma=False,
    )
```

```python
import functools

import jax
import jax.numpy as jnp
from jax import lax
from jax.experimental import pallas as pl
from jax.experimental.pallas import tpu as pltpu
from jax.sharding import PartitionSpec as P

LANES = 128
QUARTER = 16
OCEAN = 64
LABEL_ROWS = 16
MIB = 1024 * 1024
SMEM = pl.BlockSpec(memory_space=pltpu.SMEM)
VMEM = pl.BlockSpec(memory_space=pltpu.VMEM)
HBM = pl.BlockSpec(memory_space=pltpu.HBM)


def lanes_of(shape):
    return lax.broadcasted_iota(jnp.int32, shape, 1)


def params(mib):
    return pltpu.CompilerParams(vmem_limit_bytes=mib * MIB)


def edge_kernel(
    capacity,
    owner_ref,
    local_ref,
    x_ref,
    early_ref,
    late_ref,
    edge_ref,
    at_ref,
    label_ref,
    slab_ref,
    pick,
    count_ref,
    sem,
):
    rows, chan, cols = x_ref.shape
    parts = sem.shape[0]
    chunk = rows // parts

    def load(k):
        at = pl.ds(k * chunk, chunk)
        return pltpu.make_async_copy(x_ref.at[at], slab_ref.at[at], sem.at[k])

    for k in range(parts):
        load(k).start()
    shape = (cols, LANES)
    column, lane = lax.broadcasted_iota(jnp.int32, shape, 0), lanes_of(shape)
    for n in range(8):
        wanted = ((column == cols - 1) & (lane == n)) | ((column == 0) & (lane == LANES // 2 + n))
        pick[n * cols : (n + 1) * cols] = wanted.astype(jnp.float32).astype(jnp.bfloat16)

    peers = label_ref.shape[0]
    piece_rows = OCEAN * chan // LANES
    for p in range(peers):
        count_ref[p] = 0

    def assign(q, table):
        owner = owner_ref[q]
        taken = count_ref[owner]
        at_ref[q] = owner * (capacity * piece_rows + LABEL_ROWS) + taken * piece_rows
        count_ref[owner] = taken + 1
        here = (lax.broadcasted_iota(jnp.int32, table.shape, 0) == owner) & (
            lanes_of(table.shape) == taken
        )
        return jnp.where(here, local_ref[q] * 4 + q % 4, table)

    table = lax.fori_loop(
        0, owner_ref.shape[0], assign, jnp.full((peers, LANES), owner_ref.shape[0], jnp.int32)
    ).astype(jnp.float32)
    for p in range(peers):
        label_ref[p] = jnp.broadcast_to(table[p : p + 1], (LABEL_ROWS, LANES)).astype(jnp.bfloat16)

    total = jnp.zeros((chan, LANES), jnp.float32)
    for g in range(rows // 8):
        if 8 * g % chunk == 0:
            load(8 * g // chunk).wait()
        cells = jnp.concatenate([slab_ref[8 * g + n] for n in range(8)], axis=1)
        found = jnp.dot(cells, pick[...], preferred_element_type=jnp.float32)
        total = total + (pltpu.roll(found, 8 * g, 1) if g else found)
    edge_ref[...] = total.astype(jnp.bfloat16)
    last = jnp.where(is_even("rows"), rows - 1, 0)
    early_ref[...] = slab_ref[last]
    late_ref[...] = slab_ref[rows - 1 - last]


def find_edges(x, owners, locals_, peers, capacity):
    rows, chan, cols = x.shape
    row = jax.ShapeDtypeStruct((chan, cols), jnp.bfloat16)
    return pl.pallas_call(
        functools.partial(edge_kernel, capacity),
        out_shape=(
            row,
            row,
            jax.ShapeDtypeStruct((chan, LANES), jnp.bfloat16),
            jax.ShapeDtypeStruct(owners.shape, jnp.int32),
            jax.ShapeDtypeStruct((peers, LABEL_ROWS, LANES), jnp.bfloat16),
        ),
        in_specs=[SMEM, SMEM, HBM],
        out_specs=(VMEM, VMEM, VMEM, SMEM, VMEM),
        scratch_shapes=[
            pltpu.VMEM(x.shape, jnp.bfloat16),
            pltpu.VMEM((8 * cols, LANES), jnp.bfloat16),
            pltpu.SMEM((peers,), jnp.int32),
            pltpu.SemaphoreType.DMA((4,)),
        ],
        compiler_params=params(48),
        cost_estimate=pl.CostEstimate(flops=1_000_000, bytes_accessed=x.size * 2, transcendentals=0),
        name="find_edges",
    )(owners, locals_, x)


def swaps(axis):
    count = lax.axis_size(axis)
    pairs = [[(i, i + 1) for i in range(start, count - 1, 2)] for start in range(2)]
    return [some + [(b, a) for a, b in some] for some in pairs]


def is_even(axis):
    return lax.axis_index(axis) % 2 == 0


def expand(masks, rows):
    total = jnp.zeros(masks[0].shape, jnp.float32)
    for mask, row in zip(masks, rows):
        total = jnp.where(mask, row, total)
    return total.astype(jnp.bfloat16)


def split(value):
    high = value.astype(jnp.bfloat16).astype(jnp.float32)
    return high, value - high


def parts_of(w):
    value = [w[k : k + 1] for k in range(4)]
    first = [0.5 * w[4 + k : 5 + k] for k in range(4)]
    second = [0.5 * w[8 + k : 9 + k] for k in range(4)]
    return value, first, second


def fill_matrices(inner, outer, w, i):
    cols = outer.shape[0] // 2
    value, first, second = parts_of(w)
    shape = (cols, LANES)
    column = (lanes_of(shape) - 8 * i) & (LANES - 1)
    offset = lax.broadcasted_iota(jnp.int32, shape, 0) - 2 * column
    masks = [offset == 0, offset == 1, offset == -1, offset == 2]
    for s in range(2):
        across = [-first[2], -first[3]] if s == 0 else [first[0], first[1]]
        near = split(value[2 * s] + across[0] - second[2 * s + 1])
        far = split(value[2 * s + 1] + across[1] + second[2 * s])
        at = slice(s * cols, (s + 1) * cols)
        inner[at, 0:LANES] = expand(masks, [near[0], far[0], -second[2 * s], second[2 * s + 1]])
        inner[at, LANES:] = expand(masks[:2], [near[1], far[1]])
    outer[0:cols] = expand(masks[:2], [-first[0], -first[1]])
    outer[cols:] = expand(masks[:2], [first[2], first[3]])


def side_matrix(rows_of, band):
    shape = (LANES, LANES)
    source, lane = lax.broadcasted_iota(jnp.int32, shape, 0), lanes_of(shape)
    first = QUARTER * band + 2 * (lane // 8)
    last = LANES // 2 + QUARTER * band + 2 * (((lane + 1) & (LANES - 1)) // 8)
    total = jnp.zeros(shape, jnp.float32)
    for s in range(2):
        row = jnp.zeros((1, LANES), jnp.float32)
        at = lanes_of(row.shape)
        for i in range(8):
            _, _, second = parts_of(rows_of[i])
            row = jnp.where(at == 8 * i, -second[2 * s], row)
            row = jnp.where(at == (8 * i - 1) % LANES, second[2 * s + 1], row)
        here = ((lane % 8 == 0) & (source == first + s)) | ((lane % 8 == 7) & (source == last + s))
        total = jnp.where(here, row, total)
    return total.astype(jnp.bfloat16)


def gather_quarters(held, chunk, places, out_ref):
    half = held.shape[1] // 2
    group = lanes_of((QUARTER, LANES)) // 8
    mixed = []
    for part in range(2):
        start = part * half + chunk * QUARTER
        lines = [held[i, start : start + QUARTER] for i in range(8)]
        for bit in (1, 2, 4):
            on = (group & bit) != 0
            lines = [jnp.where(on, lines[(n + bit) % 8], lines[n]) for n in range(8)]
        mixed.append(lines)
    for qc in range(8):
        lower, upper = mixed[0][-qc % 8], mixed[1][-qc % 8]
        early = ((group - qc) & 15) < 8
        both = (jnp.where(early, lower, upper), jnp.where(early, upper, lower))
        for n, piece in enumerate(both):
            turn = (LANES - 8 * qc + (n + qc) * LANES // 2) % LANES
            if turn:
                piece = pltpu.roll(piece, turn, 1)
            at = pl.multiple_of(places[qc + 8 * n] + chunk * QUARTER, QUARTER)
            out_ref[pl.ds(at, QUARTER), :] = piece.astype(jnp.bfloat16)


def piece_kernel(
    at_ref,
    choice_ref,
    label_ref,
    weight_ref,
    x_ref,
    early_ref,
    late_ref,
    early_side_ref,
    late_side_ref,
    out_ref,
    slab,
    above,
    below,
    inner,
    outer,
    weights_ref,
    held,
    sem,
):
    rows, chan, cols = x_ref.shape
    bands, across = rows // QUARTER, cols // QUARTER
    peers = label_ref.shape[0]
    peer_rows = out_ref.shape[0] // peers
    half = chan // 2
    chunks = half // QUARTER

    def load(band):
        start, stop = band * QUARTER + min(band, 1), min((band + 1) * QUARTER + 1, rows)
        cuts = [start + (stop - start) * n // 4 for n in range(5)]
        spans = [pl.ds(low, high - low) for low, high in zip(cuts[:-1], cuts[1:])]
        return [
            pltpu.make_async_copy(x_ref.at[at], slab.at[at], sem.at[band, n])
            for n, at in enumerate(spans)
        ]

    def begin(band):
        for copy in load(band):
            copy.start()

    def finish(band):
        for copy in load(band):
            copy.wait()

    begin(0)
    for p in range(peers):
        out_ref[(p + 1) * peer_rows - LABEL_ROWS : (p + 1) * peer_rows, :] = label_ref[p]

    shape = (QUARTER, LANES)
    block = lanes_of(shape) // 8
    gathered = [jnp.zeros(shape, jnp.float32) for _ in range(8)]
    empty = jnp.zeros((4, OCEAN), jnp.float32)
    for n in range(weight_ref.shape[0]):
        terms = [weight_ref[n, m].astype(jnp.float32) for m in range(3)] + [empty]
        terms = jnp.concatenate(terms, axis=0)
        terms = jnp.concatenate([terms, jnp.zeros_like(terms)], axis=1)
        for i in range(8):
            turn = (8 * n - 8 * i) % LANES
            turned = pltpu.roll(terms, turn, 1) if turn else terms
            gathered[i] = jnp.where(block == n, turned, gathered[i])
    for i in range(8):
        weights_ref[QUARTER * i : QUARTER * (i + 1), :] = gathered[i].astype(jnp.bfloat16)

    even_row = is_even("rows")
    lane = lanes_of(early_side_ref.shape)
    take_early = (lane >= LANES // 2) == is_even("cols")
    sides = jnp.where(
        take_early, early_side_ref[...].astype(jnp.float32), late_side_ref[...].astype(jnp.float32)
    ).astype(jnp.bfloat16)
    finish(0)
    begin(1)

    @pl.loop(0, bands)
    def _(band):
        for b in range(1, bands):

            @pl.when(band == b)
            def _():
                finish(b)
                if b + 1 < bands:
                    begin(b + 1)

        above[...] = slab[jnp.maximum(band * QUARTER - 1, 0)]
        below[...] = slab[jnp.minimum((band + 1) * QUARTER, rows - 1)]

        @pl.when(band == 0)
        def _():
            above[...] = jnp.where(even_row, late_ref[...], early_ref[...])

        @pl.when(band == bands - 1)
        def _():
            below[...] = jnp.where(even_row, early_ref[...], late_ref[...])

        start = (band // 2) * (across // 2) * 4 + (band % 2) * 2
        pairs = [start + (column // 2) * 4 + column % 2 for column in range(across)]

        shape = (LANES, LANES)
        wj, lane = lax.broadcasted_iota(jnp.int32, shape, 0), lanes_of(shape)
        row = (1, LANES)
        choice = jnp.zeros(row, jnp.int32)
        for column, q in enumerate(pairs):
            choice = jnp.where(lanes_of(row) // 8 == column, choice_ref[q], choice)
        pick = (wj // 8 == choice) & (wj % 8 == lane % 8)
        weights = jnp.dot(
            weights_ref[...],
            pick.astype(jnp.float32).astype(jnp.bfloat16),
            preferred_element_type=jnp.float32,
        )
        rows_of = [weights[QUARTER * i : QUARTER * (i + 1)] for i in range(8)]
        rows_of = [pltpu.roll(w, 8 * i, 1) if i else w for i, w in enumerate(rows_of)]
        beside = jnp.dot(sides, side_matrix(rows_of, band), preferred_element_type=jnp.float32)
        for i in range(8):
            fill_matrices(inner.at[i], outer.at[i], rows_of[i], i)
        for i in range(8):
            base = QUARTER * band + 2 * i
            own = jnp.dot(
                jnp.concatenate([slab[base], slab[base + 1]], axis=1),
                inner[i],
                preferred_element_type=jnp.float32,
            )
            next_to = [slab[base - 1] if i else above[...], slab[base + 2] if i < 7 else below[...]]
            near = jnp.dot(
                jnp.concatenate(next_to, axis=1),
                outer[i],
                preferred_element_type=jnp.float32,
            )
            lane = lanes_of(near.shape)
            rim = (lane == 8 * i) | (lane == (8 * i - 1) % LANES)
            total = (own[:, 0:LANES] + own[:, LANES:]) + (near + jnp.where(rim, beside, 0.0))
            held[i, 0:half] = total[0:half]
            held[i, half:] = pltpu.roll(total[half:], LANES // 2, 1)

        places = [at_ref[q] for q in pairs]
        for chunk in range(chunks):
            gather_quarters(held, chunk, places, out_ref)


def make_pieces(x, halo, remap_weights, slots, labels, choices, capacity):
    rows, chan, cols = x.shape
    peers = labels.shape[0]
    bands, across = rows // QUARTER, cols // QUARTER
    piece_rows = OCEAN * chan // LANES
    return pl.pallas_call(
        piece_kernel,
        out_shape=jax.ShapeDtypeStruct(
            (peers * (capacity * piece_rows + LABEL_ROWS), LANES), jnp.bfloat16
        ),
        in_specs=[SMEM, SMEM, VMEM, VMEM, HBM, VMEM, VMEM, VMEM, VMEM],
        out_specs=VMEM,
        scratch_shapes=[
            pltpu.VMEM(x.shape, jnp.bfloat16),
            pltpu.VMEM((chan, cols), jnp.bfloat16),
            pltpu.VMEM((chan, cols), jnp.bfloat16),
            pltpu.VMEM((8, 2 * cols, 2 * LANES), jnp.bfloat16),
            pltpu.VMEM((8, 2 * cols, LANES), jnp.bfloat16),
            pltpu.VMEM((LANES, LANES), jnp.bfloat16),
            pltpu.VMEM((8, chan, LANES), jnp.float32),
            pltpu.SemaphoreType.DMA((bands, 4)),
        ],
        compiler_params=params(48),
        cost_estimate=pl.CostEstimate(
            flops=4_000_000_000, bytes_accessed=16_000_000, transcendentals=0
        ),
        name="pieces",
    )(slots, choices, labels, remap_weights, x, *halo)


def sum_kernel(capacity, arrived_ref, out_ref, stage, label_vmem, label_smem, head, after, sums, sem):
    blocks, chan, _ = out_ref.shape
    peers = label_vmem.shape[0]
    half = chan // 2
    peer_rows = arrived_ref.shape[0] // peers
    for p in range(peers):
        found = arrived_ref[(p + 1) * peer_rows - LABEL_ROWS : (p + 1) * peer_rows, :]
        label_vmem[p : p + 1] = found.astype(jnp.float32)[0:1].astype(jnp.int32)
    copy = pltpu.make_async_copy(label_vmem, label_smem, sem)
    copy.start()
    head[4 * blocks] = -1

    @pl.loop(0, 4 * blocks, unroll=8)
    def _(t):
        head[t] = -1

    copy.wait()

    @pl.loop(0, peers, unroll=4)
    def _(p):
        for k in range(capacity):
            target = label_smem[p, k]
            slot = p * (peer_rows // 16) + k * (half // 16)
            after[slot] = head[target]
            head[target] = slot

    early = lanes_of((half, LANES)) < LANES // 2

    some = sums.shape[0] // 4

    @pl.loop(0, blocks // some)
    def _(group):
        @pl.loop(0, 4 * some)
        def _(n):
            def more(held):
                return held[0] >= 0

            def add(held):
                slot, total = held
                piece = arrived_ref[pl.ds(pl.multiple_of(slot * 16, 16), half), :]
                return after[slot], total + piece.astype(jnp.float32)

            start = (head[group * 4 * some + n], jnp.zeros((half, LANES), jnp.float32))
            sums[n] = lax.while_loop(more, add, start)[1]

        for n in range(some):
            block = group * some + n
            for pair in range(2):
                first, second = sums[4 * n + 2 * pair], sums[4 * n + 2 * pair + 1]
                lower, upper = jnp.where(early, first, second), jnp.where(early, second, first)
                at = slice(pair * LANES, (pair + 1) * LANES)
                stage[block, 0:half, at] = lower.astype(jnp.bfloat16)
                stage[block, half:, at] = pltpu.roll(upper, LANES // 2, 1).astype(jnp.bfloat16)
            pltpu.make_async_copy(stage.at[block], out_ref.at[block], sem).start()

    pltpu.make_async_copy(stage, out_ref, sem).wait()


def sum_arrived(arrived, blocks, chan, peers, capacity):
    return pl.pallas_call(
        functools.partial(sum_kernel, capacity),
        out_shape=jax.ShapeDtypeStruct((blocks, chan, 4 * OCEAN), jnp.bfloat16),
        in_specs=[VMEM],
        out_specs=HBM,
        scratch_shapes=[
            pltpu.VMEM((blocks, chan, 4 * OCEAN), jnp.bfloat16),
            pltpu.VMEM((peers, LANES), jnp.int32),
            pltpu.SMEM((peers, LANES), jnp.int32),
            pltpu.SMEM((4 * blocks + 1,), jnp.int32),
            pltpu.SMEM((arrived.shape[0] // 16,), jnp.int32),
            pltpu.VMEM((16, chan // 2, LANES), jnp.float32),
            pltpu.SemaphoreType.DMA,
        ],
        compiler_params=params(8),
        cost_estimate=pl.CostEstimate(flops=10_000_000, bytes_accessed=8_000_000, transcendentals=0),
        name="sum_arrived",
    )(arrived)


def per_device(atm_field, remap_weights, pair_owner, pair_local, pair_weight):
    rows, cols, chan = atm_field.shape
    pairs = pair_local.shape[0]
    peers = lax.axis_size("rows")
    capacity = 2 * pairs // peers
    x = atm_field.transpose(0, 2, 1)
    owners = pair_owner[:, 0]
    early, late, edge, slots, labels = find_edges(x, owners, pair_local, peers, capacity)
    halo = [lax.ppermute(row, "rows", swap) for row, swap in zip((early, late), swaps("rows"))]
    halo += [lax.ppermute(edge, "cols", swap) for swap in swaps("cols")]
    outgoing = make_pieces(
        x,
        halo,
        remap_weights,
        slots,
        labels,
        pair_weight,
        capacity,
    )
    outgoing = outgoing.reshape(peers, -1, LANES)
    arrived = lax.all_to_all(outgoing, "rows", split_axis=0, concat_axis=0, tiled=True)
    arrived = arrived.reshape(-1, LANES)
    return sum_arrived(arrived, pairs // 4, chan, peers, capacity).transpose(0, 2, 1)


def solution(mesh):
    placed = (
        P("rows", "cols", None),
        P(("rows", "cols"), None, None, None),
        P(("rows", "cols"), None),
        P(("rows", "cols")),
        P(("rows", "cols")),
    )
    return jax.shard_map(
        per_device,
        mesh=mesh,
        in_specs=placed,
        out_specs=P(("rows", "cols"), None, None),
        check_vma=False,
    )
```

```python
import functools

import jax
import jax.numpy as jnp
from jax import lax
from jax.experimental import pallas as pl
from jax.experimental.pallas import tpu as pltpu
from jax.sharding import PartitionSpec as P

LANES = 128
QUARTER = 16
OCEAN = 64
LABEL_ROWS = 16
MIB = 1024 * 1024
SMEM = pl.BlockSpec(memory_space=pltpu.SMEM)
VMEM = pl.BlockSpec(memory_space=pltpu.VMEM)
HBM = pl.BlockSpec(memory_space=pltpu.HBM)


def lanes_of(shape):
    return lax.broadcasted_iota(jnp.int32, shape, 1)


def params(mib):
    return pltpu.CompilerParams(vmem_limit_bytes=mib * MIB)


def edge_kernel(x_ref, early_ref, late_ref, edge_ref, slab_ref, pick, sem):
    rows, chan, cols = x_ref.shape
    parts = sem.shape[0]
    chunk = rows // parts

    def load(k):
        at = pl.ds(k * chunk, chunk)
        return pltpu.make_async_copy(x_ref.at[at], slab_ref.at[at], sem.at[k])

    for k in range(parts):
        load(k).start()
    shape = (cols, LANES)
    column, lane = lax.broadcasted_iota(jnp.int32, shape, 0), lanes_of(shape)
    for n in range(8):
        wanted = ((column == cols - 1) & (lane == n)) | ((column == 0) & (lane == LANES // 2 + n))
        pick[n * cols : (n + 1) * cols] = wanted.astype(jnp.float32).astype(jnp.bfloat16)

    total = jnp.zeros((chan, LANES), jnp.float32)
    for g in range(rows // 8):
        if 8 * g % chunk == 0:
            load(8 * g // chunk).wait()
        cells = jnp.concatenate([slab_ref[8 * g + n] for n in range(8)], axis=1)
        found = jnp.dot(cells, pick[...], preferred_element_type=jnp.float32)
        total = total + (pltpu.roll(found, 8 * g, 1) if g else found)
    edge_ref[...] = total.astype(jnp.bfloat16)
    last = jnp.where(is_even("rows"), rows - 1, 0)
    early_ref[...] = slab_ref[last]
    late_ref[...] = slab_ref[rows - 1 - last]


def find_edges(x):
    rows, chan, cols = x.shape
    row = jax.ShapeDtypeStruct((chan, cols), jnp.bfloat16)
    return pl.pallas_call(
        edge_kernel,
        out_shape=(
            row,
            row,
            jax.ShapeDtypeStruct((chan, LANES), jnp.bfloat16),
        ),
        in_specs=[HBM],
        out_specs=(VMEM, VMEM, VMEM),
        scratch_shapes=[
            pltpu.VMEM(x.shape, jnp.bfloat16),
            pltpu.VMEM((8 * cols, LANES), jnp.bfloat16),
            pltpu.SemaphoreType.DMA((4,)),
        ],
        compiler_params=params(48),
        cost_estimate=pl.CostEstimate(flops=1_000_000, bytes_accessed=x.size * 2, transcendentals=0),
        name="find_edges",
    )(x)


def swaps(axis):
    count = lax.axis_size(axis)
    pairs = [[(i, i + 1) for i in range(start, count - 1, 2)] for start in range(2)]
    return [some + [(b, a) for a, b in some] for some in pairs]


def is_even(axis):
    return lax.axis_index(axis) % 2 == 0


def expand(masks, rows):
    total = jnp.zeros(masks[0].shape, jnp.float32)
    for mask, row in zip(masks, rows):
        total = jnp.where(mask, row, total)
    return total.astype(jnp.bfloat16)


def split(value):
    high = value.astype(jnp.bfloat16).astype(jnp.float32)
    return high, value - high


def parts_of(w):
    value = [w[k : k + 1] for k in range(4)]
    first = [0.5 * w[4 + k : 5 + k] for k in range(4)]
    second = [0.5 * w[8 + k : 9 + k] for k in range(4)]
    return value, first, second


def fill_matrices(inner, outer, w, i):
    cols = outer.shape[0] // 2
    value, first, second = parts_of(w)
    shape = (cols, LANES)
    column = (lanes_of(shape) - 8 * i) & (LANES - 1)
    offset = lax.broadcasted_iota(jnp.int32, shape, 0) - 2 * column
    masks = [offset == 0, offset == 1, offset == -1, offset == 2]
    for s in range(2):
        across = [-first[2], -first[3]] if s == 0 else [first[0], first[1]]
        near = split(value[2 * s] + across[0] - second[2 * s + 1])
        far = split(value[2 * s + 1] + across[1] + second[2 * s])
        at = slice(s * cols, (s + 1) * cols)
        inner[at, 0:LANES] = expand(masks, [near[0], far[0], -second[2 * s], second[2 * s + 1]])
        inner[at, LANES:] = expand(masks[:2], [near[1], far[1]])
    outer[0:cols] = expand(masks[:2], [-first[0], -first[1]])
    outer[cols:] = expand(masks[:2], [first[2], first[3]])


def side_matrix(rows_of, band):
    shape = (LANES, LANES)
    source, lane = lax.broadcasted_iota(jnp.int32, shape, 0), lanes_of(shape)
    first = QUARTER * band + 2 * (lane // 8)
    last = LANES // 2 + QUARTER * band + 2 * (((lane + 1) & (LANES - 1)) // 8)
    total = jnp.zeros(shape, jnp.float32)
    for s in range(2):
        row = jnp.zeros((1, LANES), jnp.float32)
        at = lanes_of(row.shape)
        for i in range(8):
            _, _, second = parts_of(rows_of[i])
            row = jnp.where(at == 8 * i, -second[2 * s], row)
            row = jnp.where(at == (8 * i - 1) % LANES, second[2 * s + 1], row)
        here = ((lane % 8 == 0) & (source == first + s)) | ((lane % 8 == 7) & (source == last + s))
        total = jnp.where(here, row, total)
    return total.astype(jnp.bfloat16)


def gather_quarters(held, chunk, places, out_ref):
    half = held.shape[1] // 2
    group = lanes_of((QUARTER, LANES)) // 8
    mixed = []
    for part in range(2):
        start = part * half + chunk * QUARTER
        lines = [held[i, start : start + QUARTER] for i in range(8)]
        for bit in (1, 2, 4):
            on = (group & bit) != 0
            lines = [jnp.where(on, lines[(n + bit) % 8], lines[n]) for n in range(8)]
        mixed.append(lines)
    for qc in range(8):
        lower, upper = mixed[0][-qc % 8], mixed[1][-qc % 8]
        early = ((group - qc) & 15) < 8
        both = (jnp.where(early, lower, upper), jnp.where(early, upper, lower))
        for n, piece in enumerate(both):
            turn = (LANES - 8 * qc + (n + qc) * LANES // 2) % LANES
            if turn:
                piece = pltpu.roll(piece, turn, 1)
            at = pl.multiple_of(places[qc + 8 * n] + chunk * QUARTER, QUARTER)
            out_ref[pl.ds(at, QUARTER), :] = piece.astype(jnp.bfloat16)


def piece_kernel(
    capacity,
    owner_ref,
    local_ref,
    choice_ref,
    weight_ref,
    x_ref,
    early_ref,
    late_ref,
    early_side_ref,
    late_side_ref,
    out_ref,
    slab,
    above,
    below,
    inner,
    outer,
    weights_ref,
    held,
    at_ref,
    count_ref,
    sem,
):
    rows, chan, cols = x_ref.shape
    bands, across = rows // QUARTER, cols // QUARTER
    peers = count_ref.shape[0]
    peer_rows = out_ref.shape[0] // peers
    half = chan // 2
    chunks = half // QUARTER

    def load(band):
        start, stop = band * QUARTER + min(band, 1), min((band + 1) * QUARTER + 1, rows)
        cuts = [start + (stop - start) * n // 4 for n in range(5)]
        spans = [pl.ds(low, high - low) for low, high in zip(cuts[:-1], cuts[1:])]
        return [
            pltpu.make_async_copy(x_ref.at[at], slab.at[at], sem.at[band, n])
            for n, at in enumerate(spans)
        ]

    def begin(band):
        for copy in load(band):
            copy.start()

    def finish(band):
        for copy in load(band):
            copy.wait()

    begin(0)

    piece_rows = OCEAN * chan // LANES
    for p in range(peers):
        count_ref[p] = 0

    def assign(q, table):
        owner = owner_ref[q]
        taken = count_ref[owner]
        at_ref[q] = owner * (capacity * piece_rows + LABEL_ROWS) + taken * piece_rows
        count_ref[owner] = taken + 1
        here = (lax.broadcasted_iota(jnp.int32, table.shape, 0) == owner) & (
            lanes_of(table.shape) == taken
        )
        return jnp.where(here, local_ref[q] * 4 + q % 4, table)

    table = lax.fori_loop(
        0, owner_ref.shape[0], assign, jnp.full((peers, LANES), owner_ref.shape[0], jnp.int32)
    ).astype(jnp.float32)
    for p in range(peers):
        label = jnp.broadcast_to(table[p : p + 1], (LABEL_ROWS, LANES)).astype(jnp.bfloat16)
        out_ref[(p + 1) * peer_rows - LABEL_ROWS : (p + 1) * peer_rows, :] = label

    shape = (QUARTER, LANES)
    block = lanes_of(shape) // 8
    gathered = [jnp.zeros(shape, jnp.float32) for _ in range(8)]
    empty = jnp.zeros((4, OCEAN), jnp.float32)
    for n in range(weight_ref.shape[0]):
        terms = [weight_ref[n, m].astype(jnp.float32) for m in range(3)] + [empty]
        terms = jnp.concatenate(terms, axis=0)
        terms = jnp.concatenate([terms, jnp.zeros_like(terms)], axis=1)
        for i in range(8):
            turn = (8 * n - 8 * i) % LANES
            turned = pltpu.roll(terms, turn, 1) if turn else terms
            gathered[i] = jnp.where(block == n, turned, gathered[i])
    for i in range(8):
        weights_ref[QUARTER * i : QUARTER * (i + 1), :] = gathered[i].astype(jnp.bfloat16)

    even_row = is_even("rows")
    lane = lanes_of(early_side_ref.shape)
    take_early = (lane >= LANES // 2) == is_even("cols")
    sides = jnp.where(
        take_early, early_side_ref[...].astype(jnp.float32), late_side_ref[...].astype(jnp.float32)
    ).astype(jnp.bfloat16)
    finish(0)
    begin(1)

    @pl.loop(0, bands)
    def _(band):
        for b in range(1, bands):

            @pl.when(band == b)
            def _():
                finish(b)
                if b + 1 < bands:
                    begin(b + 1)

        above[...] = slab[jnp.maximum(band * QUARTER - 1, 0)]
        below[...] = slab[jnp.minimum((band + 1) * QUARTER, rows - 1)]

        @pl.when(band == 0)
        def _():
            above[...] = jnp.where(even_row, late_ref[...], early_ref[...])

        @pl.when(band == bands - 1)
        def _():
            below[...] = jnp.where(even_row, early_ref[...], late_ref[...])

        start = (band // 2) * (across // 2) * 4 + (band % 2) * 2
        pairs = [start + (column // 2) * 4 + column % 2 for column in range(across)]

        shape = (LANES, LANES)
        wj, lane = lax.broadcasted_iota(jnp.int32, shape, 0), lanes_of(shape)
        row = (1, LANES)
        choice = jnp.zeros(row, jnp.int32)
        for column, q in enumerate(pairs):
            choice = jnp.where(lanes_of(row) // 8 == column, choice_ref[q], choice)
        pick = (wj // 8 == choice) & (wj % 8 == lane % 8)
        weights = jnp.dot(
            weights_ref[...],
            pick.astype(jnp.float32).astype(jnp.bfloat16),
            preferred_element_type=jnp.float32,
        )
        rows_of = [weights[QUARTER * i : QUARTER * (i + 1)] for i in range(8)]
        rows_of = [pltpu.roll(w, 8 * i, 1) if i else w for i, w in enumerate(rows_of)]
        beside = jnp.dot(sides, side_matrix(rows_of, band), preferred_element_type=jnp.float32)
        for i in range(8):
            fill_matrices(inner.at[i], outer.at[i], rows_of[i], i)
        for i in range(8):
            base = QUARTER * band + 2 * i
            own = jnp.dot(
                jnp.concatenate([slab[base], slab[base + 1]], axis=1),
                inner[i],
                preferred_element_type=jnp.float32,
            )
            next_to = [slab[base - 1] if i else above[...], slab[base + 2] if i < 7 else below[...]]
            near = jnp.dot(
                jnp.concatenate(next_to, axis=1),
                outer[i],
                preferred_element_type=jnp.float32,
            )
            lane = lanes_of(near.shape)
            rim = (lane == 8 * i) | (lane == (8 * i - 1) % LANES)
            total = (own[:, 0:LANES] + own[:, LANES:]) + (near + jnp.where(rim, beside, 0.0))
            held[i, 0:half] = total[0:half]
            held[i, half:] = pltpu.roll(total[half:], LANES // 2, 1)

        places = [at_ref[q] for q in pairs]
        for chunk in range(chunks):
            gather_quarters(held, chunk, places, out_ref)


def make_pieces(x, halo, remap_weights, owners, locals_, choices, peers, capacity):
    rows, chan, cols = x.shape
    bands, across = rows // QUARTER, cols // QUARTER
    piece_rows = OCEAN * chan // LANES
    return pl.pallas_call(
        functools.partial(piece_kernel, capacity),
        out_shape=jax.ShapeDtypeStruct(
            (peers * (capacity * piece_rows + LABEL_ROWS), LANES), jnp.bfloat16
        ),
        in_specs=[SMEM, SMEM, SMEM, VMEM, HBM, VMEM, VMEM, VMEM, VMEM],
        out_specs=VMEM,
        scratch_shapes=[
            pltpu.VMEM(x.shape, jnp.bfloat16),
            pltpu.VMEM((chan, cols), jnp.bfloat16),
            pltpu.VMEM((chan, cols), jnp.bfloat16),
            pltpu.VMEM((8, 2 * cols, 2 * LANES), jnp.bfloat16),
            pltpu.VMEM((8, 2 * cols, LANES), jnp.bfloat16),
            pltpu.VMEM((LANES, LANES), jnp.bfloat16),
            pltpu.VMEM((8, chan, LANES), jnp.float32),
            pltpu.SMEM(owners.shape, jnp.int32),
            pltpu.SMEM((peers,), jnp.int32),
            pltpu.SemaphoreType.DMA((bands, 4)),
        ],
        compiler_params=params(48),
        cost_estimate=pl.CostEstimate(
            flops=4_000_000_000, bytes_accessed=16_000_000, transcendentals=0
        ),
        name="pieces",
    )(owners, locals_, choices, remap_weights, x, *halo)


def sum_kernel(capacity, arrived_ref, out_ref, stage, label_vmem, label_smem, head, after, sums, sem):
    blocks, chan, _ = out_ref.shape
    peers = label_vmem.shape[0]
    half = chan // 2
    peer_rows = arrived_ref.shape[0] // peers
    for p in range(peers):
        found = arrived_ref[(p + 1) * peer_rows - LABEL_ROWS : (p + 1) * peer_rows, :]
        label_vmem[p : p + 1] = found.astype(jnp.float32)[0:1].astype(jnp.int32)
    copy = pltpu.make_async_copy(label_vmem, label_smem, sem)
    copy.start()
    head[4 * blocks] = -1

    @pl.loop(0, 4 * blocks, unroll=8)
    def _(t):
        head[t] = -1

    copy.wait()

    @pl.loop(0, peers, unroll=4)
    def _(p):
        for k in range(capacity):
            target = label_smem[p, k]
            slot = p * (peer_rows // 16) + k * (half // 16)
            after[slot] = head[target]
            head[target] = slot

    early = lanes_of((half, LANES)) < LANES // 2

    some = sums.shape[0] // 4

    @pl.loop(0, blocks // some)
    def _(group):
        @pl.loop(0, 4 * some)
        def _(n):
            def more(held):
                return held[0] >= 0

            def add(held):
                slot, total = held
                piece = arrived_ref[pl.ds(pl.multiple_of(slot * 16, 16), half), :]
                return after[slot], total + piece.astype(jnp.float32)

            start = (head[group * 4 * some + n], jnp.zeros((half, LANES), jnp.float32))
            sums[n] = lax.while_loop(more, add, start)[1]

        for n in range(some):
            block = group * some + n
            for pair in range(2):
                first, second = sums[4 * n + 2 * pair], sums[4 * n + 2 * pair + 1]
                lower, upper = jnp.where(early, first, second), jnp.where(early, second, first)
                at = slice(pair * LANES, (pair + 1) * LANES)
                stage[block, 0:half, at] = lower.astype(jnp.bfloat16)
                stage[block, half:, at] = pltpu.roll(upper, LANES // 2, 1).astype(jnp.bfloat16)
            pltpu.make_async_copy(stage.at[block], out_ref.at[block], sem).start()

    pltpu.make_async_copy(stage, out_ref, sem).wait()


def sum_arrived(arrived, blocks, chan, peers, capacity):
    return pl.pallas_call(
        functools.partial(sum_kernel, capacity),
        out_shape=jax.ShapeDtypeStruct((blocks, chan, 4 * OCEAN), jnp.bfloat16),
        in_specs=[VMEM],
        out_specs=HBM,
        scratch_shapes=[
            pltpu.VMEM((blocks, chan, 4 * OCEAN), jnp.bfloat16),
            pltpu.VMEM((peers, LANES), jnp.int32),
            pltpu.SMEM((peers, LANES), jnp.int32),
            pltpu.SMEM((4 * blocks + 1,), jnp.int32),
            pltpu.SMEM((arrived.shape[0] // 16,), jnp.int32),
            pltpu.VMEM((16, chan // 2, LANES), jnp.float32),
            pltpu.SemaphoreType.DMA,
        ],
        compiler_params=params(8),
        cost_estimate=pl.CostEstimate(flops=10_000_000, bytes_accessed=8_000_000, transcendentals=0),
        name="sum_arrived",
    )(arrived)


def per_device(atm_field, remap_weights, pair_owner, pair_local, pair_weight):
    rows, cols, chan = atm_field.shape
    pairs = pair_local.shape[0]
    peers = lax.axis_size("rows")
    capacity = 2 * pairs // peers
    x = atm_field.transpose(0, 2, 1)
    owners = pair_owner[:, 0]
    early, late, edge = find_edges(x)
    halo = [lax.ppermute(row, "rows", swap) for row, swap in zip((early, late), swaps("rows"))]
    halo += [lax.ppermute(edge, "cols", swap) for swap in swaps("cols")]
    outgoing = make_pieces(
        x,
        halo,
        remap_weights,
        owners,
        pair_local,
        pair_weight,
        peers,
        capacity,
    )
    outgoing = outgoing.reshape(peers, -1, LANES)
    arrived = lax.all_to_all(outgoing, "rows", split_axis=0, concat_axis=0, tiled=True)
    arrived = arrived.reshape(-1, LANES)
    return sum_arrived(arrived, pairs // 4, chan, peers, capacity).transpose(0, 2, 1)


def solution(mesh):
    placed = (
        P("rows", "cols", None),
        P(("rows", "cols"), None, None, None),
        P(("rows", "cols"), None),
        P(("rows", "cols")),
        P(("rows", "cols")),
    )
    return jax.shard_map(
        per_device,
        mesh=mesh,
        in_specs=placed,
        out_specs=P(("rows", "cols"), None, None),
        check_vma=False,
    )
```

```python
import functools

import jax
import jax.numpy as jnp
from jax import lax
from jax.experimental import pallas as pl
from jax.experimental.pallas import tpu as pltpu
from jax.sharding import PartitionSpec as P

LANES = 128
QUARTER = 16
OCEAN = 64
LABEL_ROWS = 16
MIB = 1024 * 1024
SMEM = pl.BlockSpec(memory_space=pltpu.SMEM)
VMEM = pl.BlockSpec(memory_space=pltpu.VMEM)
HBM = pl.BlockSpec(memory_space=pltpu.HBM)


def lanes_of(shape):
    return lax.broadcasted_iota(jnp.int32, shape, 1)


def params(mib):
    return pltpu.CompilerParams(vmem_limit_bytes=mib * MIB)


def edge_kernel(x_ref, early_ref, late_ref, early_side_ref, late_side_ref, slab_ref, pick, sem):
    rows, chan, cols = x_ref.shape
    parts = sem.shape[0]
    chunk = rows // parts

    def load(k):
        at = pl.ds(k * chunk, chunk)
        return pltpu.make_async_copy(x_ref.at[at], slab_ref.at[at], sem.at[k])

    for k in range(parts):
        load(k).start()
    shape = (cols, LANES)
    column, lane = lax.broadcasted_iota(jnp.int32, shape, 0), lanes_of(shape)
    for n in range(8):
        wanted = ((column == cols - 1) & (lane == n)) | ((column == 0) & (lane == LANES // 2 + n))
        pick[n * cols : (n + 1) * cols] = wanted.astype(jnp.float32).astype(jnp.bfloat16)

    total = jnp.zeros((chan, LANES), jnp.float32)
    for g in range(rows // 8):
        if 8 * g % chunk == 0:
            load(8 * g // chunk).wait()
        cells = jnp.concatenate([slab_ref[8 * g + n] for n in range(8)], axis=1)
        found = jnp.dot(cells, pick[...], preferred_element_type=jnp.float32)
        total = total + (pltpu.roll(found, 8 * g, 1) if g else found)
    half = chan // 2
    lower, upper = total[0:half], total[half:]
    turned_lower, turned_upper = (pltpu.roll(part, LANES // 2, 1) for part in (lower, upper))
    start = lanes_of(lower.shape) < LANES // 2
    last_column = jnp.where(start, lower, turned_upper)
    first_column = jnp.where(start, turned_lower, upper)
    even = is_even("cols")
    early_side_ref[...] = jnp.where(even, last_column, first_column).astype(jnp.bfloat16)
    late_side_ref[...] = jnp.where(even, first_column, last_column).astype(jnp.bfloat16)
    last = jnp.where(is_even("rows"), rows - 1, 0)
    early_ref[...] = slab_ref[last]
    late_ref[...] = slab_ref[rows - 1 - last]


def find_edges(x):
    rows, chan, cols = x.shape
    row = jax.ShapeDtypeStruct((chan, cols), jnp.bfloat16)
    side = jax.ShapeDtypeStruct((chan // 2, LANES), jnp.bfloat16)
    return pl.pallas_call(
        edge_kernel,
        out_shape=(
            row,
            row,
            side,
            side,
        ),
        in_specs=[HBM],
        out_specs=(VMEM, VMEM, VMEM, VMEM),
        scratch_shapes=[
            pltpu.VMEM(x.shape, jnp.bfloat16),
            pltpu.VMEM((8 * cols, LANES), jnp.bfloat16),
            pltpu.SemaphoreType.DMA((4,)),
        ],
        compiler_params=params(48),
        cost_estimate=pl.CostEstimate(flops=1_000_000, bytes_accessed=x.size * 2, transcendentals=0),
        name="find_edges",
    )(x)


def swaps(axis):
    count = lax.axis_size(axis)
    pairs = [[(i, i + 1) for i in range(start, count - 1, 2)] for start in range(2)]
    return [some + [(b, a) for a, b in some] for some in pairs]


def is_even(axis):
    return lax.axis_index(axis) % 2 == 0


def expand(masks, rows):
    total = jnp.zeros(masks[0].shape, jnp.float32)
    for mask, row in zip(masks, rows):
        total = jnp.where(mask, row, total)
    return total.astype(jnp.bfloat16)


def split(value):
    high = value.astype(jnp.bfloat16).astype(jnp.float32)
    return high, value - high


def parts_of(w):
    value = [w[k : k + 1] for k in range(4)]
    first = [0.5 * w[4 + k : 5 + k] for k in range(4)]
    second = [0.5 * w[8 + k : 9 + k] for k in range(4)]
    return value, first, second


def fill_matrices(inner, outer, w, i):
    cols = outer.shape[0] // 2
    value, first, second = parts_of(w)
    shape = (cols, LANES)
    column = (lanes_of(shape) - 8 * i) & (LANES - 1)
    offset = lax.broadcasted_iota(jnp.int32, shape, 0) - 2 * column
    masks = [offset == 0, offset == 1, offset == -1, offset == 2]
    for s in range(2):
        across = [-first[2], -first[3]] if s == 0 else [first[0], first[1]]
        near = split(value[2 * s] + across[0] - second[2 * s + 1])
        far = split(value[2 * s + 1] + across[1] + second[2 * s])
        at = slice(s * cols, (s + 1) * cols)
        inner[at, 0:LANES] = expand(masks, [near[0], far[0], -second[2 * s], second[2 * s + 1]])
        inner[at, LANES:] = expand(masks[:2], [near[1], far[1]])
    outer[0:cols] = expand(masks[:2], [-first[0], -first[1]])
    outer[cols:] = expand(masks[:2], [first[2], first[3]])


def side_matrix(rows_of, band):
    shape = (LANES, LANES)
    source, lane = lax.broadcasted_iota(jnp.int32, shape, 0), lanes_of(shape)
    first = QUARTER * band + 2 * (lane // 8)
    last = LANES // 2 + QUARTER * band + 2 * (((lane + 1) & (LANES - 1)) // 8)
    total = jnp.zeros(shape, jnp.float32)
    for s in range(2):
        row = jnp.zeros((1, LANES), jnp.float32)
        at = lanes_of(row.shape)
        for i in range(8):
            _, _, second = parts_of(rows_of[i])
            row = jnp.where(at == 8 * i, -second[2 * s], row)
            row = jnp.where(at == (8 * i - 1) % LANES, second[2 * s + 1], row)
        here = ((lane % 8 == 0) & (source == first + s)) | ((lane % 8 == 7) & (source == last + s))
        total = jnp.where(here, row, total)
    return total.astype(jnp.bfloat16)


def gather_quarters(held, chunk, places, out_ref):
    half = held.shape[1] // 2
    group = lanes_of((QUARTER, LANES)) // 8
    mixed = []
    for part in range(2):
        start = part * half + chunk * QUARTER
        lines = [held[i, start : start + QUARTER] for i in range(8)]
        for bit in (1, 2, 4):
            on = (group & bit) != 0
            lines = [jnp.where(on, lines[(n + bit) % 8], lines[n]) for n in range(8)]
        mixed.append(lines)
    for qc in range(8):
        lower, upper = mixed[0][-qc % 8], mixed[1][-qc % 8]
        early = ((group - qc) & 15) < 8
        both = (jnp.where(early, lower, upper), jnp.where(early, upper, lower))
        for n, piece in enumerate(both):
            turn = (LANES - 8 * qc + (n + qc) * LANES // 2) % LANES
            if turn:
                piece = pltpu.roll(piece, turn, 1)
            at = pl.multiple_of(places[qc + 8 * n] + chunk * QUARTER, QUARTER)
            out_ref[pl.ds(at, QUARTER), :] = piece.astype(jnp.bfloat16)


def piece_kernel(
    capacity,
    owner_ref,
    local_ref,
    choice_ref,
    weight_ref,
    x_ref,
    early_ref,
    late_ref,
    early_side_ref,
    late_side_ref,
    out_ref,
    slab,
    above,
    below,
    inner,
    outer,
    weights_ref,
    held,
    at_ref,
    count_ref,
    sem,
):
    rows, chan, cols = x_ref.shape
    bands, across = rows // QUARTER, cols // QUARTER
    peers = count_ref.shape[0]
    peer_rows = out_ref.shape[0] // peers
    half = chan // 2
    chunks = half // QUARTER

    def load(band):
        start, stop = band * QUARTER + min(band, 1), min((band + 1) * QUARTER + 1, rows)
        cuts = [start + (stop - start) * n // 4 for n in range(5)]
        spans = [pl.ds(low, high - low) for low, high in zip(cuts[:-1], cuts[1:])]
        return [
            pltpu.make_async_copy(x_ref.at[at], slab.at[at], sem.at[band, n])
            for n, at in enumerate(spans)
        ]

    def begin(band):
        for copy in load(band):
            copy.start()

    def finish(band):
        for copy in load(band):
            copy.wait()

    begin(0)

    piece_rows = OCEAN * chan // LANES
    for p in range(peers):
        count_ref[p] = 0

    def assign(q, table):
        owner = owner_ref[q]
        taken = count_ref[owner]
        at_ref[q] = owner * (capacity * piece_rows + LABEL_ROWS) + taken * piece_rows
        count_ref[owner] = taken + 1
        here = (lax.broadcasted_iota(jnp.int32, table.shape, 0) == owner) & (
            lanes_of(table.shape) == taken
        )
        return jnp.where(here, local_ref[q] * 4 + q % 4, table)

    table = lax.fori_loop(
        0, owner_ref.shape[0], assign, jnp.full((peers, LANES), owner_ref.shape[0], jnp.int32)
    ).astype(jnp.float32)
    for p in range(peers):
        label = jnp.broadcast_to(table[p : p + 1], (LABEL_ROWS, LANES)).astype(jnp.bfloat16)
        out_ref[(p + 1) * peer_rows - LABEL_ROWS : (p + 1) * peer_rows, :] = label

    shape = (QUARTER, LANES)
    block = lanes_of(shape) // 8
    gathered = [jnp.zeros(shape, jnp.float32) for _ in range(8)]
    empty = jnp.zeros((4, OCEAN), jnp.float32)
    for n in range(weight_ref.shape[0]):
        terms = [weight_ref[n, m].astype(jnp.float32) for m in range(3)] + [empty]
        terms = jnp.concatenate(terms, axis=0)
        terms = jnp.concatenate([terms, jnp.zeros_like(terms)], axis=1)
        for i in range(8):
            turn = (8 * n - 8 * i) % LANES
            turned = pltpu.roll(terms, turn, 1) if turn else terms
            gathered[i] = jnp.where(block == n, turned, gathered[i])
    for i in range(8):
        weights_ref[QUARTER * i : QUARTER * (i + 1), :] = gathered[i].astype(jnp.bfloat16)

    even_row = is_even("rows")
    even = is_even("cols")
    early_side, late_side = (r[...].astype(jnp.float32) for r in (early_side_ref, late_side_ref))
    west, east = jnp.where(even, late_side, early_side), jnp.where(even, early_side, late_side)
    start = lanes_of(west.shape) < LANES // 2
    sides = [
        jnp.where(start, west, pltpu.roll(east, LANES // 2, 1)),
        jnp.where(start, pltpu.roll(west, LANES // 2, 1), east),
    ]
    sides = jnp.concatenate(sides, axis=0).astype(jnp.bfloat16)
    finish(0)
    begin(1)

    @pl.loop(0, bands)
    def _(band):
        for b in range(1, bands):

            @pl.when(band == b)
            def _():
                finish(b)
                if b + 1 < bands:
                    begin(b + 1)

        above[...] = slab[jnp.maximum(band * QUARTER - 1, 0)]
        below[...] = slab[jnp.minimum((band + 1) * QUARTER, rows - 1)]

        @pl.when(band == 0)
        def _():
            above[...] = jnp.where(even_row, late_ref[...], early_ref[...])

        @pl.when(band == bands - 1)
        def _():
            below[...] = jnp.where(even_row, early_ref[...], late_ref[...])

        start = (band // 2) * (across // 2) * 4 + (band % 2) * 2
        pairs = [start + (column // 2) * 4 + column % 2 for column in range(across)]

        shape = (LANES, LANES)
        wj, lane = lax.broadcasted_iota(jnp.int32, shape, 0), lanes_of(shape)
        row = (1, LANES)
        choice = jnp.zeros(row, jnp.int32)
        for column, q in enumerate(pairs):
            choice = jnp.where(lanes_of(row) // 8 == column, choice_ref[q], choice)
        pick = (wj // 8 == choice) & (wj % 8 == lane % 8)
        weights = jnp.dot(
            weights_ref[...],
            pick.astype(jnp.float32).astype(jnp.bfloat16),
            preferred_element_type=jnp.float32,
        )
        rows_of = [weights[QUARTER * i : QUARTER * (i + 1)] for i in range(8)]
        rows_of = [pltpu.roll(w, 8 * i, 1) if i else w for i, w in enumerate(rows_of)]
        beside = jnp.dot(sides, side_matrix(rows_of, band), preferred_element_type=jnp.float32)
        for i in range(8):
            fill_matrices(inner.at[i], outer.at[i], rows_of[i], i)
        for i in range(8):
            base = QUARTER * band + 2 * i
            own = jnp.dot(
                jnp.concatenate([slab[base], slab[base + 1]], axis=1),
                inner[i],
                preferred_element_type=jnp.float32,
            )
            next_to = [slab[base - 1] if i else above[...], slab[base + 2] if i < 7 else below[...]]
            near = jnp.dot(
                jnp.concatenate(next_to, axis=1),
                outer[i],
                preferred_element_type=jnp.float32,
            )
            lane = lanes_of(near.shape)
            rim = (lane == 8 * i) | (lane == (8 * i - 1) % LANES)
            total = (own[:, 0:LANES] + own[:, LANES:]) + (near + jnp.where(rim, beside, 0.0))
            held[i, 0:half] = total[0:half]
            held[i, half:] = pltpu.roll(total[half:], LANES // 2, 1)

        places = [at_ref[q] for q in pairs]
        for chunk in range(chunks):
            gather_quarters(held, chunk, places, out_ref)


def make_pieces(x, halo, remap_weights, owners, locals_, choices, peers, capacity):
    rows, chan, cols = x.shape
    bands, across = rows // QUARTER, cols // QUARTER
    piece_rows = OCEAN * chan // LANES
    return pl.pallas_call(
        functools.partial(piece_kernel, capacity),
        out_shape=jax.ShapeDtypeStruct(
            (peers * (capacity * piece_rows + LABEL_ROWS), LANES), jnp.bfloat16
        ),
        in_specs=[SMEM, SMEM, SMEM, VMEM, HBM, VMEM, VMEM, VMEM, VMEM],
        out_specs=VMEM,
        scratch_shapes=[
            pltpu.VMEM(x.shape, jnp.bfloat16),
            pltpu.VMEM((chan, cols), jnp.bfloat16),
            pltpu.VMEM((chan, cols), jnp.bfloat16),
            pltpu.VMEM((8, 2 * cols, 2 * LANES), jnp.bfloat16),
            pltpu.VMEM((8, 2 * cols, LANES), jnp.bfloat16),
            pltpu.VMEM((LANES, LANES), jnp.bfloat16),
            pltpu.VMEM((8, chan, LANES), jnp.float32),
            pltpu.SMEM(owners.shape, jnp.int32),
            pltpu.SMEM((peers,), jnp.int32),
            pltpu.SemaphoreType.DMA((bands, 4)),
        ],
        compiler_params=params(48),
        cost_estimate=pl.CostEstimate(
            flops=4_000_000_000, bytes_accessed=16_000_000, transcendentals=0
        ),
        name="pieces",
    )(owners, locals_, choices, remap_weights, x, *halo)


def sum_kernel(capacity, arrived_ref, out_ref, stage, label_vmem, label_smem, head, after, sums, sem):
    blocks, chan, _ = out_ref.shape
    peers = label_vmem.shape[0]
    half = chan // 2
    peer_rows = arrived_ref.shape[0] // peers
    for p in range(peers):
        found = arrived_ref[(p + 1) * peer_rows - LABEL_ROWS : (p + 1) * peer_rows, :]
        label_vmem[p : p + 1] = found.astype(jnp.float32)[0:1].astype(jnp.int32)
    copy = pltpu.make_async_copy(label_vmem, label_smem, sem)
    copy.start()
    head[4 * blocks] = -1

    @pl.loop(0, 4 * blocks, unroll=8)
    def _(t):
        head[t] = -1

    copy.wait()

    @pl.loop(0, peers, unroll=4)
    def _(p):
        for k in range(capacity):
            target = label_smem[p, k]
            slot = p * (peer_rows // 16) + k * (half // 16)
            after[slot] = head[target]
            head[target] = slot

    early = lanes_of((half, LANES)) < LANES // 2

    some = sums.shape[0] // 4

    @pl.loop(0, blocks // some)
    def _(group):
        @pl.loop(0, 4 * some)
        def _(n):
            def more(held):
                return held[0] >= 0

            def add(held):
                slot, total = held
                piece = arrived_ref[pl.ds(pl.multiple_of(slot * 16, 16), half), :]
                return after[slot], total + piece.astype(jnp.float32)

            start = (head[group * 4 * some + n], jnp.zeros((half, LANES), jnp.float32))
            sums[n] = lax.while_loop(more, add, start)[1]

        for n in range(some):
            block = group * some + n
            for pair in range(2):
                first, second = sums[4 * n + 2 * pair], sums[4 * n + 2 * pair + 1]
                lower, upper = jnp.where(early, first, second), jnp.where(early, second, first)
                at = slice(pair * LANES, (pair + 1) * LANES)
                stage[block, 0:half, at] = lower.astype(jnp.bfloat16)
                stage[block, half:, at] = pltpu.roll(upper, LANES // 2, 1).astype(jnp.bfloat16)
            pltpu.make_async_copy(stage.at[block], out_ref.at[block], sem).start()

    pltpu.make_async_copy(stage, out_ref, sem).wait()


def sum_arrived(arrived, blocks, chan, peers, capacity):
    return pl.pallas_call(
        functools.partial(sum_kernel, capacity),
        out_shape=jax.ShapeDtypeStruct((blocks, chan, 4 * OCEAN), jnp.bfloat16),
        in_specs=[VMEM],
        out_specs=HBM,
        scratch_shapes=[
            pltpu.VMEM((blocks, chan, 4 * OCEAN), jnp.bfloat16),
            pltpu.VMEM((peers, LANES), jnp.int32),
            pltpu.SMEM((peers, LANES), jnp.int32),
            pltpu.SMEM((4 * blocks + 1,), jnp.int32),
            pltpu.SMEM((arrived.shape[0] // 16,), jnp.int32),
            pltpu.VMEM((16, chan // 2, LANES), jnp.float32),
            pltpu.SemaphoreType.DMA,
        ],
        compiler_params=params(8),
        cost_estimate=pl.CostEstimate(flops=10_000_000, bytes_accessed=8_000_000, transcendentals=0),
        name="sum_arrived",
    )(arrived)


def per_device(atm_field, remap_weights, pair_owner, pair_local, pair_weight):
    rows, cols, chan = atm_field.shape
    pairs = pair_local.shape[0]
    peers = lax.axis_size("rows")
    capacity = 2 * pairs // peers
    x = atm_field.transpose(0, 2, 1)
    owners = pair_owner[:, 0]
    early, late, *sides = find_edges(x)
    halo = [lax.ppermute(row, "rows", swap) for row, swap in zip((early, late), swaps("rows"))]
    halo += [lax.ppermute(side, "cols", swap) for side, swap in zip(sides, swaps("cols"))]
    outgoing = make_pieces(
        x,
        halo,
        remap_weights,
        owners,
        pair_local,
        pair_weight,
        peers,
        capacity,
    )
    outgoing = outgoing.reshape(peers, -1, LANES)
    arrived = lax.all_to_all(outgoing, "rows", split_axis=0, concat_axis=0, tiled=True)
    arrived = arrived.reshape(-1, LANES)
    return sum_arrived(arrived, pairs // 4, chan, peers, capacity).transpose(0, 2, 1)


def solution(mesh):
    placed = (
        P("rows", "cols", None),
        P(("rows", "cols"), None, None, None),
        P(("rows", "cols"), None),
        P(("rows", "cols")),
        P(("rows", "cols")),
    )
    return jax.shard_map(
        per_device,
        mesh=mesh,
        in_specs=placed,
        out_specs=P(("rows", "cols"), None, None),
        check_vma=False,
    )
```
